256 devices in a mesh: dp: 4 (over y), latent: 64 (over x, z, core).
Axes of the slice: x: 4, y: 4, z: 8, core: 2. Of those that a mesh axis runs over, the one named last changes fastest.
Arguments:
- acts: bfloat16 [32768, 8192], P(('dp', 'latent')), may hold values from -6 to 6
- blocks: int32 [32768, 2], P(('dp', 'latent')), may hold values from 0 to 191, as said below
- w_enc: bfloat16 [8192, 12288], P(None, 'latent'), may hold values from -0.0625 to 0.0625
- b_enc: float32 [12288], P('latent'), may hold values from -3 to 3
- w_dec: bfloat16 [12288, 8192], P('latent'), may hold values from -0.0625 to 0.0625
- b_dec: float32 [8192], replicated, may hold values from -3 to 3
Outputs:
- grad_w_enc: float32 [8192, 12288], P('dp', 'latent')
- grad_b_enc: float32 [12288], P('latent')
- grad_w_dec: float32 [12288, 8192], P('latent', 'dp')
The draws below stay inside these ranges and needn't reach their ends.
Inputs may be any that keep to these rules, and one draw needn't show every extreme that they name: Each row names 2 different blocks. Block b lies on index b // 3 of latent. Among the rows of one device no block is named more than 2 times and the blocks of one index of latent are named no more than 6 times in all; in every device some block is named exactly 2 times and some index of latent exactly 6 times.
All inputs are finite; a program needn't handle non-finite values.
Results may differ from the reference program's by a relative error of at most 0.004.
Values may be sent and summed in bfloat16 or wider, within the bound.
A program may use at most 128 MiB of HBM per device.

```python
import jax
import jax.numpy as jnp
from jax import lax

D = 8192
BW = 64
K = 2
BLK_DEV = 3
ROWS_DEV = 128
LATENTS = 12288
CAP = 2
OCAP = 6
ROWS = 32768
N_DP = 4
N_LATENT = 64


def device_blocks(group_key):
    keys = jax.random.split(group_key, 5)
    slots_all = N_LATENT * BLK_DEV * CAP
    pairs = ROWS_DEV * K
    owner_shift = jax.random.randint(keys[0], (N_LATENT, 1, 1), 0, BLK_DEV)
    inner = jnp.arange(BLK_DEV, dtype=jnp.int32)[None, :, None]
    column = jnp.arange(CAP, dtype=jnp.int32)[None, None, :]
    order_pos = (inner - owner_shift) % BLK_DEV
    capacity = jnp.clip(OCAP - order_pos * CAP, 0, CAP)
    valid = column < capacity
    forced = jax.random.randint(keys[1], (), 0, N_LATENT)
    owner_ids = jnp.arange(N_LATENT, dtype=jnp.int32)[:, None, None]
    level = jnp.where(valid, jnp.where(owner_ids == forced, 2, 1), 0)
    noise = jax.random.randint(keys[2], (N_LATENT, BLK_DEV, CAP), 0, 2 ** 14)
    flat_index = jnp.arange(slots_all, dtype=jnp.int32).reshape(N_LATENT, BLK_DEV, CAP)
    score = level * 2 ** 28 + noise * 8192 + flat_index
    _, chosen = lax.top_k(score.reshape(-1), pairs)
    listed = jnp.sort((chosen // CAP).astype(jnp.int32))
    table = listed.reshape(K, ROWS_DEV).T
    row_perm = jax.random.permutation(keys[3], ROWS_DEV)
    table = table[row_perm]
    roll = jax.random.randint(keys[4], (ROWS_DEV, 1), 0, K)
    take = (jnp.arange(K, dtype=jnp.int32)[None, :] + roll) % K
    return jnp.take_along_axis(table, take, axis=1).astype(jnp.int32)


def draw_blocks(key, part):
    key = jax.random.fold_in(key, 11)
    group_keys = jax.random.split(key, N_DP * N_LATENT)
    result = jax.vmap(device_blocks)(group_keys)
    return result.reshape(ROWS_DEV * N_DP * N_LATENT, K)


def block_scale(stream_key, shape, cuts, low, largest):
    level, own = 1.0, jax.random.fold_in(stream_key, 6)
    for axis_at, shards_of in cuts:
        heights = jnp.exp(jax.random.uniform(jax.random.fold_in(own, axis_at), (shards_of,), jnp.float32, low / len(cuts), largest / len(cuts)))
        level = level * jnp.repeat(heights, shape[axis_at] // shards_of).reshape([-1 if axis == axis_at else 1 for axis in range(len(shape))])
    return level


def normal_values(key, shape, deviation, bound, pieces=(), kind=jnp.bfloat16):
    values = jax.random.normal(key, shape, jnp.float32) * deviation
    if len(pieces) > 0:
        values = block_scale(key, shape, pieces, -0.22, 0.18) * values
    return jnp.clip(values, min=-bound, max=bound).astype(kind)


def setup_inputs(seed: int = 0) -> dict:
    arg_keys = jax.random.split(jax.random.key(seed), 7)
    acts = normal_values(arg_keys[0], (ROWS, D), 1.0, 6.0, ((0, 256),))
    blocks = draw_blocks(jax.random.fold_in(arg_keys[6], 71), 0)
    w_enc = normal_values(arg_keys[2], (D, LATENTS), D ** -0.5, 0.0625, ((1, 64),))
    b_enc = normal_values(arg_keys[3], (LATENTS,), 0.5, 3.0, ((0, 64),), jnp.float32)
    w_dec = normal_values(arg_keys[4], (LATENTS, D), D ** -0.5, 0.0625, ((0, 64),))
    b_dec = normal_values(arg_keys[5], (D,), 0.5, 3.0, (), jnp.float32)
    return {"acts": acts, "blocks": blocks, "w_enc": w_enc, "b_enc": b_enc, "w_dec": w_dec, "b_dec": b_dec}


def gelu_slope(value):
    return 0.5 * (1.0 + lax.erf(value * 0.7071067811865476)) + value * jnp.exp(-0.5 * value * value) * 0.3989422804014327


def reference(acts, blocks, w_enc, b_enc, w_dec, b_dec):
    rows = acts.shape[0]
    nblk = BLK_DEV * N_LATENT
    most = N_DP * N_LATENT * CAP
    flat = blocks.reshape(-1).astype(jnp.int32)
    order = jnp.argsort(flat, stable=True).astype(jnp.int32)
    counts = jnp.sum((flat[:, None] == jnp.arange(nblk, dtype=jnp.int32)[None, :]).astype(jnp.int32), axis=0)
    starts = (jnp.cumsum(counts) - counts).astype(jnp.int32)
    padded = jnp.concatenate([order, jnp.zeros((most,), jnp.int32)])

    def pick(index):
        start = starts[index]
        chosen = lax.dynamic_slice(padded, (start,), (most,))
        valid = jnp.arange(most, dtype=jnp.int32) < counts[index]
        return (chosen // K).astype(jnp.int32), valid

    def encode(index, picked):
        inputs = acts[picked]
        weight = lax.dynamic_slice_in_dim(w_enc, (index * BW).astype(jnp.int32), BW, 1)
        bias = lax.dynamic_slice_in_dim(b_enc, (index * BW).astype(jnp.int32), BW, 0)
        pre = jnp.dot(inputs, weight, preferred_element_type=jnp.float32) + bias
        return inputs, pre

    def decoder_rows(index):
        return lax.dynamic_slice_in_dim(w_dec, (index * BW).astype(jnp.int32), BW, 0)

    def forward(recon, index):
        picked, valid = pick(index)
        inputs, pre = encode(index, picked)
        code = jax.nn.gelu(pre, approximate=False).astype(jnp.bfloat16)
        part = jnp.dot(code, decoder_rows(index), preferred_element_type=jnp.float32).astype(jnp.bfloat16)
        part = lax.optimization_barrier(part).astype(jnp.float32)
        part = jnp.where(valid[:, None], part, jnp.float32(0.0))
        return recon.at[picked].add(part), None

    indices = jnp.arange(nblk, dtype=jnp.int32)
    recon, _ = lax.scan(forward, jnp.zeros((rows, D), jnp.float32), indices)
    err = recon + b_dec - acts.astype(jnp.float32)
    errors = err.astype(jnp.bfloat16)

    def backward(index):
        picked, valid = pick(index)
        inputs, pre = encode(index, picked)
        code = jax.nn.gelu(pre, approximate=False).astype(jnp.bfloat16)
        wanted = jnp.where(valid[:, None], errors[picked], jnp.zeros((), jnp.bfloat16))
        decoder = decoder_rows(index)
        g_code = jnp.dot(wanted, decoder.T, preferred_element_type=jnp.float32)
        g_pre = g_code * gelu_slope(pre)
        enc_part = jnp.dot(inputs.T, g_pre.astype(jnp.bfloat16), preferred_element_type=jnp.float32)
        dec_part = jnp.dot(code.T, wanted, preferred_element_type=jnp.float32)
        return enc_part, jnp.sum(g_pre, axis=0), dec_part

    enc_all, bias_all, dec_all = lax.map(backward, indices)
    grad_w_enc = jnp.transpose(enc_all, (1, 0, 2)).reshape(D, nblk * BW)
    grad_b_enc = bias_all.reshape(nblk * BW)
    grad_w_dec = dec_all.reshape(nblk * BW, D)
    return grad_w_enc, grad_b_enc, grad_w_dec
```

```python
import functools

import jax
import jax.numpy as jnp
from jax import lax
from jax.experimental import pallas as pl
from jax.experimental.pallas import tpu as pltpu
from jax.sharding import PartitionSpec as P

F32, BF16 = jnp.float32, jnp.bfloat16
MESH = pl.DeviceIdType.MESH
ANY = pl.BlockSpec(memory_space=pl.ANY)
VMEM = pl.BlockSpec(memory_space=pltpu.VMEM)

NY, NX, NZ = 4, 4, 8
NP = NX * NZ
ROWS, D, BW, LOCAL = 128, 8192, 64, 192
DS = D // NP
SLOTS = NP * 6
LINES = NP * 3
BIG = 60 * 1024 * 1024
G_KIND = F32
PARTS = 2
PART = LINES // PARTS


def place():
    y, l = lax.axis_index("dp"), lax.axis_index("latent")
    return y, lax.div(l, 2), lax.rem(l, 2)


def shifted(p, step):
    x = lax.rem(lax.div(p, NZ) + lax.div(step, NZ), NX)
    z = lax.rem(lax.rem(p, NZ) + lax.rem(step, NZ), NZ)
    return x * NZ + z


def pair_of(p):
    return lax.div(p, 2 * NZ) * NZ + lax.rem(p, NZ)


def remote(src, dst, send, recv, device):
    return pltpu.make_async_remote_copy(
        src_ref=src, dst_ref=dst, send_sem=send, recv_sem=recv, device_id=device, device_id_type=MESH
    )


def wait_bytes(ref, sem):
    pltpu.make_async_copy(ref, ref, sem).wait()


def halves_of(v0, v1):
    return (jnp.concatenate([v0[:, 0:BW], v1[:, 0:BW]], axis=1),
            jnp.concatenate([v0[:, BW:128], v1[:, BW:128]], axis=1))


def by_chip(src, dst):
    def tile(t, _):
        v = [src[:, pl.ds(pl.multiple_of(q * (D // NY) + t * 128, 128), 128)].astype(F32) for q in range(NY)]
        even, odd = zip(halves_of(v[0], v[1]), halves_of(v[2], v[3]))
        for side, (e, o) in enumerate(((even[0], odd[0]), (even[1], odd[1]))):
            chip = lax.div(t, NZ) * 2 * NZ + lax.rem(t, NZ)
            dst[chip, :, pl.ds(side * 128, 128)] = e.astype(BF16)
            dst[chip + NZ, :, pl.ds(side * 128, 128)] = o.astype(BF16)
        return 0

    lax.fori_loop(0, NP // 2, tile, 0)


def spread_kernel(acts, info, w_enc, w_dec, acts_all, info_all, enc_all, dec_all,
                  own, own_acts, acts_cut, enc_cut, dec_cut, local_sem, send_sem, acts_sem, info_sem, enc_sem, dec_sem,
                  pair_sem, info_pair_sem, y_sem, far_sem, y_send):
    y, p, c = place()
    rows = pl.ds(pl.multiple_of(y * 48, 16), 48)
    loads = [pltpu.make_async_copy(w_enc.at[rows, :], own.at[0], local_sem.at[0]),
             pltpu.make_async_copy(w_dec.at[rows, :], own.at[1], local_sem.at[1]),
             pltpu.make_async_copy(acts, own_acts, local_sem.at[2])]
    for load in loads:
        load.start()
    barrier = pltpu.get_barrier_semaphore()

    def greet(i, _):
        pl.semaphore_signal(barrier, inc=1, device_id=(y, shifted(p, i) * 2 + c), device_id_type=MESH)
        return 0

    lax.fori_loop(1, NP, greet, 0)
    pl.semaphore_signal(barrier, inc=1, device_id=(y, p * 2 + 1 - c), device_id_type=MESH)
    for j in range(1, NY):
        pl.semaphore_signal(barrier, inc=1, device_id=(lax.rem(y + j, NY), p * 2 + c), device_id_type=MESH)
    loads[0].wait()
    by_chip(own.at[0], enc_cut)
    loads[1].wait()
    by_chip(own.at[1], dec_cut)
    pl.semaphore_wait(barrier, NP - 1 + 1 + NY - 1)

    mine = lax.div(p, NZ)
    pltpu.make_async_copy(enc_cut.at[p], enc_all.at[p, rows, :], enc_sem.at[mine]).start()
    pltpu.make_async_copy(dec_cut.at[p], dec_all.at[p, rows, :], dec_sem.at[mine]).start()
    pltpu.make_async_copy(info, info_all.at[c, p], info_sem.at[0]).start()

    def send_w(i, _):
        q = shifted(p, i)
        remote(enc_cut.at[q], enc_all.at[p, rows, :], send_sem.at[0], enc_sem.at[mine], (y, q * 2 + c)).start()
        remote(dec_cut.at[q], dec_all.at[p, rows, :], send_sem.at[1], dec_sem.at[mine], (y, q * 2 + c)).start()
        return 0

    lax.fori_loop(1, NP, send_w, 0)
    loads[2].wait()
    by_chip(own_acts, acts_cut)
    pltpu.make_async_copy(acts_cut.at[p], acts_all.at[c, p], acts_sem.at[mine]).start()

    def send_a(i, _):
        q = shifted(p, i)
        remote(info, info_all.at[c, p], send_sem.at[3], info_sem.at[0], (y, q * 2 + c)).start()
        remote(acts_cut.at[q], acts_all.at[c, p], send_sem.at[2], acts_sem.at[mine], (y, q * 2 + c)).start()
        return 0

    lax.fori_loop(1, NP, send_a, 0)

    up, down = lax.rem(y + 1, NY), lax.rem(y + NY - 1, NY)
    weights = ((enc_all, enc_sem, 0), (dec_all, dec_sem, 1))

    def pass_own(g):
        for ref, sem, n in weights:
            part = ref.at[pl.ds(g * NZ, NZ), rows, :]
            wait_bytes(part, sem.at[g])
            for side, v in enumerate((up, down)):
                remote(part, part, y_send.at[n], y_sem.at[n, side, g], (v, p * 2 + c)).start()

    def pass_on(g):
        for ref, _, n in weights:
            for side, (v, to) in enumerate(((down, up), (up, down))):
                theirs = pl.ds(pl.multiple_of(v * 48, 16), 48)
                wait_bytes(ref.at[pl.ds(g * NZ, NZ), theirs, :], y_sem.at[n, side, g])
                part = ref.at[pl.ds(g * NZ + side * (NZ // 2), NZ // 2), theirs, :]
                remote(part, part, y_send.at[n], far_sem.at[n, side], (to, p * 2 + c)).start()

    for i in range(NX + 1):
        if i < NX:
            pass_own(lax.rem(mine - i + NX, NX))
        if i > 0:
            pass_on(lax.rem(mine - i + 1 + NX, NX))
    pair = (y, p * 2 + 1 - c)
    wait_bytes(info_all.at[c], info_sem.at[0])
    remote(info_all.at[c], info_all.at[c], send_sem.at[4], info_pair_sem.at[0], pair).start()
    for i in range(NX):
        g = lax.rem(mine - i + NX, NX)
        part = acts_all.at[c, pl.ds(g * NZ, NZ)]
        wait_bytes(part, acts_sem.at[g])
        remote(part, part, send_sem.at[5], pair_sem.at[0], pair).start()

    wait_bytes(info_all.at[c], info_pair_sem.at[0])
    wait_bytes(acts_all.at[c], pair_sem.at[0])
    for n, ref in ((0, enc_all), (1, dec_all)):
        for side in range(2):
            wait_bytes(enc_cut.at[pl.ds(0, NP // 2)], far_sem.at[n, side])
        wait_bytes(ref.at[:, pl.ds(0, 144), :], y_send.at[n])
        wait_bytes(enc_cut.at[pl.ds(0, NP - 1)], send_sem.at[n])
    most = pl.ds(0, NP - 1)
    wait_bytes(acts_cut.at[most], send_sem.at[2])
    wait_bytes(info_all.at[0, most], send_sem.at[3])
    wait_bytes(info_all.at[0], send_sem.at[4])
    wait_bytes(acts_cut, send_sem.at[5])


def spread(acts, info, w_enc, w_dec):
    dma = pltpu.SemaphoreType.DMA
    return pl.pallas_call(
        spread_kernel,
        out_shape=(
            jax.ShapeDtypeStruct((2, NP, ROWS, DS), BF16),
            jax.ShapeDtypeStruct((2, NP, 16, 128), BF16),
            jax.ShapeDtypeStruct((NP, LOCAL, DS), BF16),
            jax.ShapeDtypeStruct((NP, LOCAL, DS), BF16),
        ),
        in_specs=[ANY] * 4,
        out_specs=(ANY,) * 4,
        scratch_shapes=[pltpu.VMEM((2, 48, D), BF16), pltpu.VMEM((ROWS, D), BF16),
                        pltpu.VMEM((NP, ROWS, DS), BF16), pltpu.VMEM((NP, 48, DS), BF16), pltpu.VMEM((NP, 48, DS), BF16),
                        dma((3,)), dma((6,)), dma((NX,)), dma((1,)), dma((NX,)), dma((NX,)), dma((1,)), dma((1,)),
                        dma((2, 2, NX)), dma((2, 2)), dma((2,))],
        compiler_params=pltpu.CompilerParams(collective_id=0, has_side_effects=True, vmem_limit_bytes=BIG),
        name="spread",
    )(acts, info, w_enc, w_dec)


def picks(info, c):
    half = c.astype(F32)
    slot = lax.broadcasted_iota(jnp.int32, (SLOTS, ROWS), 0).astype(F32)
    first = jnp.where(info[2:3] == half, info[0:1], -1.0)
    second = jnp.where(info[3:4] == half, info[1:2], -1.0)
    return ((slot == first) | (slot == second)).astype(F32).astype(BF16)


def low_half(shape):
    return lax.broadcasted_iota(jnp.int32, shape, 1) < BW


def lines_of(out):
    low = low_half((64, 128))
    a = jnp.where(low, out[0:64, 0:128], out[128:192, 0:128])
    b = jnp.where(low, out[64:128, 0:128], out[192:256, 0:128])
    d = jnp.concatenate([out[256:320, 128:192], out[320:384, 128:192]], axis=1)
    return a, b, d


def wide_of(a, b, d):
    low = low_half((64, 128))
    zero = jnp.zeros_like(a)
    top = jnp.concatenate(
        [jnp.where(low, a, zero), jnp.where(low, b, zero), jnp.where(low, zero, a), jnp.where(low, zero, b),
         zero, zero], axis=0)
    side = jnp.concatenate(
        [jnp.zeros((256, BW), a.dtype), d[:, 0:BW], d[:, BW:128]], axis=0)
    return jnp.concatenate([top, side], axis=1)


def store_by_slot(ref, s, value):
    ref[0, pl.ds(s, SLOTS, stride=64), :] = value[:, 0:128]
    ref[1, pl.ds(s, SLOTS, stride=64), :] = value[:, 128:256]


def load_owner(ref, o):
    rows = pl.ds(pl.multiple_of(o * 384, 384), 384)
    return jnp.concatenate([ref[0, rows, :], ref[1, rows, :]], axis=1)


def lines_out(lines, part, first, count):
    def body(s, _):
        part[s] = lines[pl.ds(s, LINES, stride=64), :].astype(part.dtype)
        return 0

    lax.fori_loop(first, first + count, body, 0, unroll=8)


def put_lines(lines, o, values):
    for k in range(3):
        lines[pl.ds(pl.multiple_of(o * 192 + k * 64, 64), 64), :] = values[k]


def get_lines(lines, o):
    return [lines[pl.ds(pl.multiple_of(o * 192 + k * 64, 64), 64), :] for k in range(3)]


def turn_in(source, lines):
    def body(s, _):
        lines[pl.ds(s, LINES, stride=64), :] = source[s].astype(F32)
        return 0

    lax.fori_loop(0, 64, body, 0, unroll=8)


CHUNKS = 4
S_STEP, O_STEP = 64 // CHUNKS, NP // CHUNKS
CHUNK_SEMS = pltpu.SemaphoreType.DMA((CHUNKS,))


def stream(src, dst, sems):
    k = src.shape[0] // CHUNKS
    return [pltpu.make_async_copy(src.at[pl.ds(i * k, k)], dst.at[pl.ds(i * k, k)], sems.at[i]) for i in range(CHUNKS)]


def start_all(*streams):
    for copies in streams:
        for copy in copies:
            copy.start()


def wait_all(*streams):
    for copies in streams:
        for copy in copies:
            copy.wait()


def encode_kernel(info_all, acts_hbm, enc_hbm, slots_hbm, part_hbm,
                  acts_all, enc_all, slots_out, part, slots, lines, a_sem, w_sem, s_sem, p_sem):
    _, _, c = place()
    acts_in, enc_in = stream(acts_hbm, acts_all, a_sem), stream(enc_hbm, enc_all, w_sem)
    out_slots, out_part = stream(slots_out, slots_hbm, s_sem), stream(part, part_hbm, p_sem)
    start_all(acts_in, enc_in)

    def expand(s, _):
        take = picks(info_all[s].astype(F32), c)
        store_by_slot(slots, s, jnp.dot(take, acts_all[s], preferred_element_type=F32))
        return 0

    def owner(o, _):
        inputs = load_owner(slots, o).astype(BF16)
        slots_out[o] = inputs
        put_lines(lines, o, lines_of(lax.dot_general(
            inputs, enc_all[o], (((1,), (1,)), ((), ())), preferred_element_type=F32)))
        return 0

    for i in range(CHUNKS):
        acts_in[i].wait()
        lax.fori_loop(i * S_STEP, (i + 1) * S_STEP, expand, 0, unroll=8)
    for i in range(CHUNKS):
        enc_in[i].wait()
        lax.fori_loop(i * O_STEP, (i + 1) * O_STEP, owner, 0, unroll=8)
        out_slots[i].start()
    for i in range(CHUNKS):
        lines_out(lines, part, i * S_STEP, S_STEP)
        out_part[i].start()
    wait_all(out_slots, out_part)


def encode(info_all, acts_all, enc_all):
    return pl.pallas_call(
        encode_kernel,
        out_shape=(
            jax.ShapeDtypeStruct((NP, 384, DS), BF16),
            jax.ShapeDtypeStruct((64, LINES, 128), F32),
        ),
        in_specs=[VMEM, ANY, ANY],
        out_specs=(ANY,) * 2,
        scratch_shapes=[pltpu.VMEM((64, ROWS, DS), BF16), pltpu.VMEM((NP, LOCAL, DS), BF16),
                        pltpu.VMEM((NP, 384, DS), BF16), pltpu.VMEM((64, LINES, 128), F32),
                        pltpu.VMEM((2, SLOTS * 64, 128), F32), pltpu.VMEM((LINES * 64, 128), F32)] + [CHUNK_SEMS] * 4,
        compiler_params=pltpu.CompilerParams(vmem_limit_bytes=BIG),
        name="encode",
    )(info_all, acts_all, enc_all)


def decode_kernel(info_all, codes, dec_hbm, recon_hbm, other_hbm, wide_hbm,
                  dec_all, recon, wide_out, slots, lines, w_sem, r_sem, o_sem, send_sem, recv_sem):
    y, p, c = place()
    pair = (y, p * 2 + 1 - c)
    barrier = pltpu.get_barrier_semaphore()
    pl.semaphore_signal(barrier, inc=1, device_id=pair, device_id_type=MESH)
    dec_in = stream(dec_hbm, dec_all, w_sem)
    out_recon, out_wide = stream(recon, recon_hbm, r_sem), stream(wide_out, wide_hbm, o_sem)
    start_all(dec_in)
    turn_in(codes, lines)

    def owner(o, _):
        wide = wide_of(*get_lines(lines, o)).astype(BF16)
        wide_out[o] = wide
        part = jnp.dot(wide, dec_all[o], preferred_element_type=F32)
        rows = pl.ds(pl.multiple_of(o * 384, 384), 384)
        slots[0, rows, :] = part[:, 0:128]
        slots[1, rows, :] = part[:, 128:256]
        return 0

    def gather(s, _):
        take = picks(info_all[s].astype(F32), c)
        part = jnp.concatenate(
            [slots[h, pl.ds(s, SLOTS, stride=64), :].astype(BF16) for h in range(2)], axis=1)
        recon[s] = lax.dot_general(
            take, part, (((0,), (0,)), ((), ())), preferred_element_type=F32).astype(BF16)
        return 0

    for i in range(CHUNKS):
        dec_in[i].wait()
        lax.fori_loop(i * O_STEP, (i + 1) * O_STEP, owner, 0, unroll=8)
        out_wide[i].start()
    pl.semaphore_wait(barrier, 1)
    sent = []
    for i in range(CHUNKS):
        lax.fori_loop(i * S_STEP, (i + 1) * S_STEP, gather, 0, unroll=8)
        out_recon[i].start()
        rows = pl.ds(i * S_STEP, S_STEP)
        sent.append(remote(recon.at[rows], other_hbm.at[rows], send_sem.at[i], recv_sem.at[i], pair))
        sent[i].start()
    wait_all(out_recon, out_wide, sent)


def decode(info_all, codes, dec_all):
    return pl.pallas_call(
        decode_kernel,
        out_shape=(
            jax.ShapeDtypeStruct((64, ROWS, DS), BF16),
            jax.ShapeDtypeStruct((64, ROWS, DS), BF16),
            jax.ShapeDtypeStruct((NP, 384, LOCAL), BF16),
        ),
        in_specs=[VMEM, VMEM, ANY],
        out_specs=(ANY,) * 3,
        scratch_shapes=[pltpu.VMEM((NP, LOCAL, DS), BF16), pltpu.VMEM((64, ROWS, DS), BF16),
                        pltpu.VMEM((NP, 384, LOCAL), BF16),
                        pltpu.VMEM((2, SLOTS * 64, 128), F32), pltpu.VMEM((LINES * 64, 128), F32)] + [CHUNK_SEMS] * 5,
        compiler_params=pltpu.CompilerParams(collective_id=4, has_side_effects=True, vmem_limit_bytes=BIG),
        name="decode",
    )(info_all, codes, dec_all)


def pack_owners(out, i, v0, v1):
    h, u = lax.div(i, 8), lax.rem(i, 8)
    for side in range(2):
        tile = slice(side * 128, side * 128 + 128)
        low, high = halves_of(v0[:, tile], v1[:, tile])
        out[2 * side, h, u] = low.astype(BF16)
        out[2 * side + 1, h, u] = high.astype(BF16)


OVER_ROWS = (((0,), (0,)), ((), ()))


def errors_kernel(info_all, b_dec, acts_hbm, mine_hbm, other_hbm, dec_hbm, wide_hbm, part, dec,
                  acts_all, mine, other, dec_all, wide, slots, lines, *sems):
    _, _, c = place()
    ins = [stream(src, dst, sem) for src, dst, sem in zip(
        (acts_hbm, mine_hbm, other_hbm, dec_hbm, wide_hbm), (acts_all, mine, other, dec_all, wide), sems)]
    for i in range(CHUNKS):
        start_all([copies[i] for copies in ins[0:3]])
    start_all(*ins[3:])

    def expand(s, _):
        recon = mine[s].astype(F32) + other[s].astype(F32)
        errors = (recon + b_dec[0:1] - acts_all[s].astype(F32)).astype(BF16)
        take = picks(info_all[s].astype(F32), c)
        store_by_slot(slots, s, jnp.dot(take, errors, preferred_element_type=F32))
        return 0

    def product(o):
        wanted = load_owner(slots, o).astype(BF16)
        grad = lax.dot_general(wanted, dec_all[o], (((1,), (1,)), ((), ())), preferred_element_type=F32)
        put_lines(lines, o, lines_of(grad))
        return lax.dot_general(wide[o], wanted, OVER_ROWS, preferred_element_type=F32)

    def owners(i, _):
        pack_owners(dec, i, product(2 * i), product(2 * i + 1))
        return 0

    for i in range(CHUNKS):
        wait_all([copies[i] for copies in ins[0:3]])
        lax.fori_loop(i * S_STEP, (i + 1) * S_STEP, expand, 0, unroll=8)
    for i in range(CHUNKS):
        wait_all([copies[i] for copies in ins[3:]])
        lax.fori_loop(i * O_STEP // 2, (i + 1) * O_STEP // 2, owners, 0, unroll=4)
    lines_out(lines, part, 0, 64)


def errors_of(info_all, acts_all, mine, other, b_dec, dec_all, wide, kind):
    return pl.pallas_call(
        errors_kernel,
        out_shape=(
            jax.ShapeDtypeStruct((64, LINES, 128), kind),
            jax.ShapeDtypeStruct((NY, 2, 8, LOCAL, 128), BF16),
        ),
        in_specs=[VMEM] * 2 + [ANY] * 5,
        out_specs=(VMEM,) * 2,
        scratch_shapes=[pltpu.VMEM((64, ROWS, DS), BF16)] * 3
        + [pltpu.VMEM((NP, LOCAL, DS), BF16), pltpu.VMEM((NP, 384, LOCAL), BF16),
           pltpu.VMEM((2, SLOTS * 64, 128), F32), pltpu.VMEM((LINES * 64, 128), F32)] + [CHUNK_SEMS] * 5,
        compiler_params=pltpu.CompilerParams(vmem_limit_bytes=BIG),
        name="errors",
    )(info_all, b_dec, acts_all, mine, other, dec_all, wide)


def enc_grads_kernel(g_all, inputs_hbm, enc, bias, inputs, lines, i_sem):
    inputs_in = stream(inputs_hbm, inputs, i_sem)
    start_all(inputs_in)
    turn_in(g_all, lines)

    def product(o):
        a, b, d = get_lines(lines, o)
        bias[o] = jnp.concatenate(
            [jnp.sum(a + b, axis=0, keepdims=True), jnp.sum(d, axis=0, keepdims=True), jnp.zeros((6, 128), F32)], axis=0)
        return lax.dot_general(wide_of(a, b, d).astype(BF16), inputs[o], OVER_ROWS, preferred_element_type=F32)

    def owners(i, _):
        pack_owners(enc, i, product(2 * i), product(2 * i + 1))
        return 0

    for i in range(CHUNKS):
        inputs_in[i].wait()
        lax.fori_loop(i * O_STEP // 2, (i + 1) * O_STEP // 2, owners, 0, unroll=4)


def enc_grads(g_all, inputs):
    return pl.pallas_call(
        enc_grads_kernel,
        out_shape=(
            jax.ShapeDtypeStruct((NY, 2, 8, LOCAL, 128), BF16),
            jax.ShapeDtypeStruct((NP, 8, 128), F32),
        ),
        in_specs=[VMEM, ANY],
        out_specs=(VMEM,) * 2,
        scratch_shapes=[pltpu.VMEM((NP, 384, DS), BF16), pltpu.VMEM((LINES * 64, 128), F32), CHUNK_SEMS],
        compiler_params=pltpu.CompilerParams(vmem_limit_bytes=BIG),
        name="enc_grads",
    )(g_all, inputs)


def meet_peers(y, p, c):
    side = lax.rem(lax.div(p, NZ), 2)

    def at(v, h):
        return (v, (p + (h - side) * NZ) * 2 + c)

    return side, lax.rem(y + 1, NY), lax.rem(y + NY - 1, NY), lax.rem(y + 2, NY), at


def meet_greet(y, p, c, barrier):
    side, up, down, far, at = meet_peers(y, p, c)
    for v in (up, down, far):
        for h in range(2):
            pl.semaphore_signal(barrier, inc=1, device_id=at(v, h), device_id_type=MESH)


MEET_PARTS = 2
MEET_ROWS = LOCAL // MEET_PARTS


def meet_rows(n):
    return pl.ds(n * MEET_ROWS, MEET_ROWS)


def meet_start(y, p, c, src, land, relay, send, recv):
    side, up, down, far, at = meet_peers(y, p, c)
    low, high = pl.ds(0, 4), pl.ds(4, 4)
    for n in range(MEET_PARTS):
        rows = meet_rows(n)
        remote(src.at[far, :, low, rows], relay.at[0, :, :, rows], send.at[0], recv.at[n, 0], at(up, side)).start()
        remote(src.at[far, :, high, rows], relay.at[1, :, :, rows], send.at[0], recv.at[n, 1], at(down, side)).start()
        for h in range(2):
            remote(src.at[up, h, high, rows], land.at[side, 1, high, rows], send.at[1], recv.at[n, 2], at(up, h)).start()
            remote(src.at[down, h, low, rows], land.at[side, 2, low, rows], send.at[1], recv.at[n, 2],
                   at(down, h)).start()
        pltpu.make_async_copy(src.at[y, side, :, rows], land.at[side, 0, :, rows], recv.at[n, 2]).start()
        remote(src.at[y, 1 - side, :, rows], land.at[side, 0, :, rows], send.at[1], recv.at[n, 2],
               at(y, 1 - side)).start()


def meet_merge(y, p, c, n, src, land, relay, merged, send, recv):
    side, up, down, far, at = meet_peers(y, p, c)
    rows = meet_rows(n)
    for k, (v, first) in enumerate(((up, 0), (down, 4))):
        wait_bytes(relay.at[k, :, :, rows], recv.at[n, k])
        for h in range(2):

            def add(i, _):
                merged[k, h, i, rows] = (
                    src[v, h, first + i, rows].astype(F32) + relay[k, h, i, rows].astype(F32)).astype(BF16)
                return 0

            lax.fori_loop(0, 4, add, 0)
            remote(merged.at[k, h, :, rows], land.at[side, 1 + k, pl.ds(first, 4), rows], send.at[1], recv.at[n, 2],
                   at(v, h)).start()


def meet_wait(n, land, recv):
    wait_bytes(land.at[:, :, :, meet_rows(n)], recv.at[n, 2])


def meet_sum(land, total, u, n):
    def tile(t, _):
        rows = pl.ds(pl.multiple_of(n * MEET_ROWS + t * 32, 32), 32)
        v = [land[e, 0, u, rows, :].astype(F32) + land[e, 1, u, rows, :].astype(F32) + land[e, 2, u, rows, :].astype(F32)
             for e in range(2)]
        low, high = halves_of(v[0], v[1])
        total[2 * u, rows, :], total[2 * u + 1, rows, :] = low.astype(BF16), high.astype(BF16)
        return 0

    lax.fori_loop(0, MEET_ROWS // 32, tile, 0)


def meet_end(land, relay, send):
    wait_bytes(relay, send.at[0])
    wait_bytes(land.at[0], send.at[1])
    wait_bytes(land.at[0, 0], send.at[1])
    wait_bytes(land.at[0, 0], send.at[1])


MEET_SCRATCH = [pltpu.VMEM((2, 3, 8, LOCAL, 128), BF16), pltpu.VMEM((2, 2, 4, LOCAL, 128), BF16),
                pltpu.VMEM((2, 2, 4, LOCAL, 128), BF16), pltpu.SemaphoreType.DMA((2,)), pltpu.SemaphoreType.DMA((MEET_PARTS, 3))]


def slope_of(v):
    return 0.5 * (1.0 + lax.erf(v * 0.7071067811865476)) + v * jnp.exp(-0.5 * v * v) * 0.3989422804014327


def exchange_kernel(forward, part, extra, *rest):
    if forward:
        (out_all, slope_out, got, code, x_relay, x_merged, x_land, z_out, send_sem, xr_sem, xl_sem, recv_sem,
         line_sem, x_sem, far_sem, back_sem) = rest
    else:
        (dec, out_all, dec_total, got, code, x_relay, x_merged, x_land, z_out, send_sem, xr_sem, xl_sem, recv_sem,
         line_sem, x_sem, far_sem, back_sem, land, relay, merged, m_send, m_recv) = rest
    y, p, c = place()
    x, z = lax.div(p, NZ), lax.rem(p, NZ)
    barrier = pltpu.get_barrier_semaphore()

    right, left = lax.rem(x + 1, NX), lax.rem(x + NX - 1, NX)
    far = lax.rem(x + 2, NX)

    def in_line(i):
        return lax.rem(z + lax.rem(i, NZ), NZ), lax.rem(c + lax.div(i, NZ), 2)

    def greet(i, _):
        w, h = in_line(i)
        pl.semaphore_signal(barrier, inc=1, device_id=(y, (x * NZ + w) * 2 + h), device_id_type=MESH)
        return 0

    lax.fori_loop(1, 2 * NZ, greet, 0)
    for v in (right, left):
        pl.semaphore_signal(barrier, inc=1, device_id=(y, (v * NZ + z) * 2 + c), device_id_type=MESH)
    if not forward:
        meet_greet(y, p, c, barrier)
    pl.semaphore_wait(barrier, 17 if forward else 23)

    def beside(v):
        return (y, (v * NZ + z) * 2 + c)

    def cut(ref, n):
        return ref.at[..., pl.ds(n * PART, PART), :]

    def rows_of(v, k, n):
        return part.at[k, pl.ds(v * NZ, NZ), pl.ds(n * PART, PART)]

    ways = ((right, left, 0), (left, right, 1))
    for n in range(PARTS):
        for to, _, k in ways:
            remote(rows_of(far, k, n), cut(x_relay.at[k], n), send_sem.at[0], xr_sem.at[n, k], beside(to)).start()
        for to, _, k in ways:
            remote(rows_of(to, 1 - k, n), cut(x_land.at[k, 1 - k], n), send_sem.at[1], xl_sem.at[n], beside(to)).start()
    for n in range(PARTS):
        own = pl.ds(n * PART, PART)
        for to, _, k in ways:
            wait_bytes(cut(x_relay.at[k], n), xr_sem.at[n, k])

            def merge(w, _):
                x_merged[k, w, own] = (
                    part[k, to * NZ + w, own].astype(F32) + x_relay[k, w, own].astype(F32)).astype(part.dtype)
                return 0

            lax.fori_loop(0, NZ, merge, 0)
            remote(cut(x_merged.at[k], n), cut(x_land.at[k, k], n), send_sem.at[1], xl_sem.at[n], beside(to)).start()
    for n in range(PARTS):
        own = pl.ds(n * PART, PART)
        wait_bytes(cut(x_land, n), xl_sem.at[n])

        def z_send(i, _):
            w, h = in_line(i)
            z_out[h, w, own] = (part[h, x * NZ + w, own].astype(F32) + x_land[0, h, w, own].astype(F32)
                                + x_land[1, h, w, own].astype(F32))
            source, target = z_out.at[h, w, own], got.at[c, z, own]

            @pl.when(i > 0)
            def _():
                remote(source, target, send_sem.at[2], recv_sem.at[n], (y, (x * NZ + w) * 2 + h)).start()

            @pl.when(i == 0)
            def _():
                pltpu.make_async_copy(source, target, recv_sem.at[n]).start()

            return 0

        lax.fori_loop(0, 2 * NZ, z_send, 0)

    if not forward:
        meet_start(y, p, c, dec, land, relay, m_send, m_recv)

    for n in range(PARTS):
        own = pl.ds(n * PART, PART)
        wait_bytes(cut(got, n), recv_sem.at[n])
        for h in range(2):
            for t in range(PART // 16):
                rows = pl.ds(n * PART + t * 16, 16)
                total = got[h, 0, rows, :]
                for q in range(1, NZ):
                    total = total + got[h, q, rows, :]
                if forward:
                    pre = total + extra[h, rows, :]
                    slope_out[h, rows, :] = slope_of(pre)
                    code[h, rows, :] = (pre * 0.5 * (1.0 + lax.erf(pre * 0.7071067811865476))).astype(BF16)
                else:
                    code[h, rows, :] = (total * extra[h, rows, :]).astype(BF16)
        pltpu.make_async_copy(code.at[c, own], out_all.at[c, p, own], line_sem.at[n]).start()

        def share(i, _):
            w, h = in_line(i)
            remote(code.at[h, own], out_all.at[c, p, own], back_sem.at[0], line_sem.at[n],
                   (y, (x * NZ + w) * 2 + h)).start()
            return 0

        lax.fori_loop(1, 2 * NZ, share, 0)

    if not forward:
        for n in range(MEET_PARTS):
            meet_merge(y, p, c, n, dec, land, relay, merged, m_send, m_recv)

    def line(v, k, n):
        return out_all.at[k, pl.ds(v * NZ, NZ), pl.ds(n * PART, PART)]

    for n in range(PARTS):
        wait_bytes(cut(out_all.at[:, pl.ds(0, NZ)], n), line_sem.at[n])
        for side, v in enumerate((right, left)):
            for k in (side, 1 - side):
                remote(line(x, k, n), line(x, k, n), back_sem.at[1], x_sem.at[n, side, k], beside(v)).start()
    for n in range(PARTS):
        for side, (v, to) in enumerate(((left, right), (right, left))):
            wait_bytes(line(v, side, n), x_sem.at[n, side, side])
            remote(line(v, side, n), line(v, side, n), back_sem.at[2], far_sem.at[n, side], beside(to)).start()
    if not forward:
        for n in range(MEET_PARTS):
            meet_wait(n, land, m_recv)

            def total_of(u, _):
                meet_sum(land, dec_total, u, n)
                return 0

            lax.fori_loop(0, 8, total_of, 0)
    for n in range(PARTS):
        for side, v in enumerate((left, right)):
            wait_bytes(line(v, 1 - side, n), x_sem.at[n, side, 1 - side])
            wait_bytes(line(v, 0, n), far_sem.at[n, side])
    wait_bytes(x_relay, send_sem.at[0])
    wait_bytes(x_land, send_sem.at[1])
    wait_bytes(got.at[0], send_sem.at[2])
    wait_bytes(got.at[0, pl.ds(0, NZ - 1)], send_sem.at[2])
    wait_bytes(out_all.at[0, pl.ds(0, 2 * NZ - 1)], back_sem.at[0])
    wait_bytes(out_all.at[0], back_sem.at[1])
    wait_bytes(out_all.at[0, pl.ds(0, 2 * NZ)], back_sem.at[2])
    if not forward:
        meet_end(land, relay, m_send)


def exchange(forward, part, extra, *dec):
    dma = pltpu.SemaphoreType.DMA
    out = [jax.ShapeDtypeStruct((2, NP, LINES, 128), BF16)]
    if forward:
        out.append(jax.ShapeDtypeStruct((2, LINES, 128), F32))
    else:
        out.append(jax.ShapeDtypeStruct((16, LOCAL, 128), BF16))
    return pl.pallas_call(
        functools.partial(exchange_kernel, forward),
        out_shape=tuple(out),
        in_specs=[VMEM] * (2 + len(dec)),
        out_specs=(VMEM,) * len(out),
        scratch_shapes=[pltpu.VMEM((2, NZ, LINES, 128), F32), pltpu.VMEM((2, LINES, 128), BF16),
                        pltpu.VMEM((2, NZ, LINES, 128), part.dtype), pltpu.VMEM((2, NZ, LINES, 128), part.dtype),
                        pltpu.VMEM((2, 2, NZ, LINES, 128), part.dtype), pltpu.VMEM((2, NZ, LINES, 128), F32),
                        dma((3,)), dma((PARTS, 2)), dma((PARTS,)), dma((PARTS,)), dma((PARTS,)), dma((PARTS, 2, 2)),
                        dma((PARTS, 2)), dma((3,))]
        + ([] if forward else MEET_SCRATCH),
        compiler_params=pltpu.CompilerParams(
            collective_id=1 if forward else 2, has_side_effects=True, vmem_limit_bytes=BIG),
        name="exchange_code" if forward else "exchange_grad",
    )(part.reshape(2, NP, LINES, 128), extra, *dec)


def deliver_kernel(enc, dec_total, bias, enc_out, dec_out, bias_out, bias_y, enc_total, b_send, b_recv,
                   send_sem, recv_sem, land, relay, merged, m_send, m_recv):
    y, p, c = place()
    x, z = lax.div(p, NZ), lax.rem(p, NZ)
    side = lax.rem(x, 2)
    barrier = pltpu.get_barrier_semaphore()

    def greet(i, _):
        pl.semaphore_signal(barrier, inc=1, device_id=(y, shifted(p, i) * 2 + c), device_id_type=MESH)
        return 0

    lax.fori_loop(1, NP, greet, 0)
    meet_greet(y, p, c, barrier)
    pl.semaphore_wait(barrier, NP - 1 + 6)

    here = pair_of(p)

    def to_owners(total, out, n, u, rows):
        for e in range(2):
            o = side * 2 * NZ + 2 * u + e

            @pl.when(o != p)
            def _():
                remote(total.at[2 * u + e, rows], out.at[here, rows], send_sem.at[n], recv_sem.at[n], (y, o * 2 + c)).start()

            @pl.when(o == p)
            def _():
                pltpu.make_async_copy(total.at[2 * u + e, rows], out.at[here, rows], recv_sem.at[n]).start()

    def turned(i):
        return lax.rem(i + lax.div(z, 2), 8)

    meet_start(y, p, c, enc, land, relay, m_send, m_recv)
    pltpu.make_async_copy(bias.at[p], bias_y.at[y], b_recv.at[0]).start()
    for j in range(1, NY):
        remote(bias.at[p], bias_y.at[y], b_send.at[0], b_recv.at[0], (lax.rem(y + j, NY), p * 2 + c)).start()

    def dec_owner(i, _):
        to_owners(dec_total, dec_out, 0, turned(i), pl.ds(0, LOCAL))
        return 0

    lax.fori_loop(0, 8, dec_owner, 0)
    for n in range(MEET_PARTS):
        meet_merge(y, p, c, n, enc, land, relay, merged, m_send, m_recv)
    for n in range(MEET_PARTS):
        meet_wait(n, land, m_recv)

        def enc_owner(i, _):
            u = turned(i)
            meet_sum(land, enc_total, u, n)
            to_owners(enc_total, enc_out, 1, u, meet_rows(n))
            return 0

        lax.fori_loop(0, 8, enc_owner, 0)
    wait_bytes(bias_y, b_recv.at[0])
    bias_out[...] = bias_y[0] + bias_y[1] + bias_y[2] + bias_y[3]
    wait_bytes(bias_y.at[pl.ds(0, NY - 1)], b_send.at[0])
    meet_end(land, relay, m_send)
    for n in range(2):
        wait_bytes(enc_total, recv_sem.at[n])
        wait_bytes(enc_total.at[pl.ds(0, 15)], send_sem.at[n])

        @pl.when(lax.div(x, 2) != side)
        def _():
            wait_bytes(enc_total.at[0], send_sem.at[n])


def deliver(enc, dec_total, bias):
    dma = pltpu.SemaphoreType.DMA
    return pl.pallas_call(
        deliver_kernel,
        out_shape=(
            jax.ShapeDtypeStruct((16, LOCAL, 128), BF16),
            jax.ShapeDtypeStruct((16, LOCAL, 128), BF16),
            jax.ShapeDtypeStruct((8, 128), F32),
        ),
        in_specs=[VMEM, VMEM, ANY],
        out_specs=(ANY, ANY, VMEM),
        scratch_shapes=[pltpu.VMEM((NY, 8, 128), F32), pltpu.VMEM((16, LOCAL, 128), BF16),
                        dma((1,)), dma((1,)), dma((2,)), dma((2,))] + MEET_SCRATCH,
        compiler_params=pltpu.CompilerParams(collective_id=3, has_side_effects=True, vmem_limit_bytes=BIG),
        name="deliver",
    )(enc, dec_total, bias)


def info_kernel(blocks, b_enc, out):
    numbers = blocks[...]
    first, second = numbers[0:1].astype(F32), numbers[1:2].astype(F32)
    square = (ROWS, ROWS)
    before = lax.broadcasted_iota(jnp.int32, square, 0) < lax.broadcasted_iota(jnp.int32, square, 1)
    first_down = jnp.transpose(jnp.broadcast_to(first, square))
    second_down = jnp.transpose(jnp.broadcast_to(second, square))

    def count(hit):
        return jnp.sum(jnp.where(hit, 1, 0), axis=0, keepdims=True)

    rank = jnp.concatenate([
        count((first_down == first) & before),
        count(first_down == second) + count((second_down == second) & before)], axis=0)
    owner = lax.div(numbers, 3)
    slot = (lax.div(owner, 2) * 3 + lax.rem(numbers, 3)) * 2 + rank
    bias = b_enc[...]
    line = jnp.concatenate(
        [bias[:, 0:128], bias[:, 0:128], jnp.concatenate([bias[:, 128:192], bias[:, 128:192]], axis=1)], axis=0)
    top = line.astype(BF16).astype(F32)
    middle = (line - top).astype(BF16).astype(F32)
    out[...] = jnp.concatenate(
        [slot.astype(F32), lax.rem(owner, 2).astype(F32), top, middle, line - top - middle, jnp.zeros((3, ROWS), F32)],
        axis=0).astype(BF16)


def info_of(blocks, b_enc):
    return pl.pallas_call(
        info_kernel,
        out_shape=jax.ShapeDtypeStruct((16, ROWS), BF16),
        in_specs=[VMEM] * 2,
        out_specs=VMEM,
        name="info",
    )(blocks.T, b_enc.reshape(1, LOCAL))


def shards(acts, blocks, w_enc, b_enc, w_dec, b_dec):
    l = lax.axis_index("latent")
    p = l // 2
    acts_all, info_all, enc_all, dec_all = spread(acts, info_of(blocks, b_enc), w_enc.T, w_dec)
    acts_all = acts_all.reshape(64, ROWS, DS)
    info_all = info_all.reshape(64, 16, 128)
    inputs, part = encode(info_all, acts_all, enc_all)
    bias = info_all.astype(F32)
    bias = (bias[:, 4:7] + bias[:, 7:10] + bias[:, 10:13]).reshape(2, LINES, 128)
    codes, slope = exchange(True, part, bias)
    recon, other, wide = decode(info_all, codes.reshape(64, LINES, 128), dec_all)
    my_b_dec = lax.dynamic_slice(b_dec.reshape(NY, D // NY), (0, pair_of(p) * 128 + p // NZ % 2 * 64), (NY, 64))
    my_b_dec = jnp.broadcast_to(my_b_dec.reshape(1, DS), (8, DS))
    g_part, dec = errors_of(info_all, acts_all, recon, other, my_b_dec, dec_all, wide, G_KIND)
    g_all, dec_total = exchange(False, g_part, slope, dec)
    enc, bias_sum = enc_grads(g_all.reshape(64, LINES, 128), inputs)
    enc_tiles, dec_tiles, lines = deliver(enc, dec_total, bias_sum)
    grad_b_enc = jnp.concatenate([lines[0], lines[1, 0:64] + lines[1, 64:128]])

    def whole(tiles):
        return tiles.transpose(1, 0, 2).reshape(LOCAL, D // NY).astype(F32)

    return whole(enc_tiles).T, grad_b_enc, whole(dec_tiles)


def solution(mesh):
    return jax.shard_map(
        shards,
        mesh=mesh,
        in_specs=(
            P(("dp", "latent"), None),
            P(("dp", "latent"), None),
            P(None, "latent"),
            P("latent"),
            P("latent", None),
            P(),
        ),
        out_specs=(P("dp", "latent"), P("latent"), P("latent", "dp")),
        check_vma=False,
    )
```

```python
import functools

import jax
import jax.numpy as jnp
from jax import lax
from jax.experimental import pallas as pl
from jax.experimental.pallas import tpu as pltpu
from jax.sharding import PartitionSpec as P

F32, BF16 = jnp.float32, jnp.bfloat16
MESH = pl.DeviceIdType.MESH
ANY = pl.BlockSpec(memory_space=pl.ANY)
VMEM = pl.BlockSpec(memory_space=pltpu.VMEM)

NY, NX, NZ = 4, 4, 8
NP = NX * NZ
ROWS, D, BW, LOCAL = 128, 8192, 64, 192
DS = D // NP
SLOTS = NP * 6
LINES = NP * 3
BIG = 60 * 1024 * 1024
G_KIND = F32
PARTS = 3
PART = LINES // PARTS


def place():
    y, l = lax.axis_index("dp"), lax.axis_index("latent")
    return y, lax.div(l, 2), lax.rem(l, 2)


def shifted(p, step):
    x = lax.rem(lax.div(p, NZ) + lax.div(step, NZ), NX)
    z = lax.rem(lax.rem(p, NZ) + lax.rem(step, NZ), NZ)
    return x * NZ + z


def pair_of(p):
    return lax.div(p, 2 * NZ) * NZ + lax.rem(p, NZ)


def remote(src, dst, send, recv, device):
    return pltpu.make_async_remote_copy(
        src_ref=src, dst_ref=dst, send_sem=send, recv_sem=recv, device_id=device, device_id_type=MESH
    )


def wait_bytes(ref, sem):
    pltpu.make_async_copy(ref, ref, sem).wait()


def halves_of(v0, v1):
    return (jnp.concatenate([v0[:, 0:BW], v1[:, 0:BW]], axis=1),
            jnp.concatenate([v0[:, BW:128], v1[:, BW:128]], axis=1))


def by_chip(src, dst):
    def tile(t, _):
        v = [src[:, pl.ds(pl.multiple_of(q * (D // NY) + t * 128, 128), 128)].astype(F32) for q in range(NY)]
        even, odd = zip(halves_of(v[0], v[1]), halves_of(v[2], v[3]))
        for side, (e, o) in enumerate(((even[0], odd[0]), (even[1], odd[1]))):
            chip = lax.div(t, NZ) * 2 * NZ + lax.rem(t, NZ)
            dst[chip, :, pl.ds(side * 128, 128)] = e.astype(BF16)
            dst[chip + NZ, :, pl.ds(side * 128, 128)] = o.astype(BF16)
        return 0

    lax.fori_loop(0, NP // 2, tile, 0)


def brought(y):
    return pl.ds(pl.multiple_of(y * 48, 16), 48)


def bring(y, p, c, cut, ref, send, recv):
    target = ref.at[p, brought(y), :]
    sem = recv.at[lax.div(p, NZ)]
    pltpu.make_async_copy(cut.at[p], target, sem).start()

    def body(i, _):
        q = shifted(p, i)
        remote(cut.at[q], target, send, sem, (y, q * 2 + c)).start()
        return 0

    lax.fori_loop(1, NP, body, 0)


def pass_own(y, p, c, ref, g, recv, y_send, y_sem):
    part = ref.at[pl.ds(g * NZ, NZ), brought(y), :]
    wait_bytes(part, recv.at[g])
    for side, step in enumerate((1, NY - 1)):
        remote(part, part, y_send.at[0], y_sem.at[side, g], (lax.rem(y + step, NY), p * 2 + c)).start()


def pass_on(y, p, c, ref, g, y_send, y_sem, far_sem):
    up, down = lax.rem(y + 1, NY), lax.rem(y + NY - 1, NY)
    for side, (v, to) in enumerate(((down, up), (up, down))):
        wait_bytes(ref.at[pl.ds(g * NZ, NZ), brought(v), :], y_sem.at[side, g])
        part = ref.at[pl.ds(g * NZ + side * (NZ // 2), NZ // 2), brought(v), :]
        remote(part, part, y_send.at[0], far_sem.at[side], (to, p * 2 + c)).start()


def bring_end(cut, ref, send, y_send, far_sem):
    for side in range(2):
        wait_bytes(cut.at[pl.ds(0, NP // 2)], far_sem.at[side])
    wait_bytes(ref.at[:, pl.ds(0, 144), :], y_send.at[0])
    wait_bytes(cut.at[pl.ds(0, NP - 1)], send)


def bring_sems():
    dma = pltpu.SemaphoreType.DMA
    return [dma((1,)), dma((NX,)), dma((1,)), dma((2, NX)), dma((2,))]


def spread_kernel(acts, info, w_enc, w_dec, acts_all, info_all, enc_all, dec_cut,
                  own, own_acts, acts_cut, enc_cut, local_sem, send_sem, acts_sem, info_sem,
                  pair_sem, info_pair_sem, w_send, w_recv, y_send, y_sem, far_sem):
    y, p, c = place()
    rows = brought(y)
    loads = [pltpu.make_async_copy(w_enc.at[rows, :], own.at[0], local_sem.at[0]),
             pltpu.make_async_copy(w_dec.at[rows, :], own.at[1], local_sem.at[1]),
             pltpu.make_async_copy(acts, own_acts, local_sem.at[2])]
    for load in loads:
        load.start()
    barrier = pltpu.get_barrier_semaphore()

    def greet(i, _):
        pl.semaphore_signal(barrier, inc=1, device_id=(y, shifted(p, i) * 2 + c), device_id_type=MESH)
        return 0

    lax.fori_loop(1, NP, greet, 0)
    pl.semaphore_signal(barrier, inc=1, device_id=(y, p * 2 + 1 - c), device_id_type=MESH)
    for j in range(1, NY):
        pl.semaphore_signal(barrier, inc=1, device_id=(lax.rem(y + j, NY), p * 2 + c), device_id_type=MESH)
    loads[0].wait()
    by_chip(own.at[0], enc_cut)
    pl.semaphore_wait(barrier, NP - 1 + 1 + NY - 1)

    mine = lax.div(p, NZ)
    pltpu.make_async_copy(info, info_all.at[c, p], info_sem.at[0]).start()

    bring(y, p, c, enc_cut, enc_all, w_send.at[0], w_recv)
    loads[2].wait()
    by_chip(own_acts, acts_cut)
    pltpu.make_async_copy(acts_cut.at[p], acts_all.at[c, p], acts_sem.at[mine]).start()

    def send_a(i, _):
        q = shifted(p, i)
        remote(info, info_all.at[c, p], send_sem.at[1], info_sem.at[0], (y, q * 2 + c)).start()
        remote(acts_cut.at[q], acts_all.at[c, p], send_sem.at[0], acts_sem.at[mine], (y, q * 2 + c)).start()
        return 0

    lax.fori_loop(1, NP, send_a, 0)

    loads[1].wait()
    by_chip(own.at[1], dec_cut)
    for i in range(NX + 1):
        if i < NX:
            pass_own(y, p, c, enc_all, lax.rem(mine - i + NX, NX), w_recv, y_send, y_sem)
        if i > 0:
            pass_on(y, p, c, enc_all, lax.rem(mine - i + 1 + NX, NX), y_send, y_sem, far_sem)
    pair = (y, p * 2 + 1 - c)
    wait_bytes(info_all.at[c], info_sem.at[0])
    remote(info_all.at[c], info_all.at[c], send_sem.at[2], info_pair_sem.at[0], pair).start()
    for i in range(NX):
        g = lax.rem(mine - i + NX, NX)
        part = acts_all.at[c, pl.ds(g * NZ, NZ)]
        wait_bytes(part, acts_sem.at[g])
        remote(part, part, send_sem.at[3], pair_sem.at[0], pair).start()

    wait_bytes(info_all.at[c], info_pair_sem.at[0])
    wait_bytes(acts_all.at[c], pair_sem.at[0])
    bring_end(enc_cut, enc_all, w_send.at[0], y_send, far_sem)
    most = pl.ds(0, NP - 1)
    wait_bytes(acts_cut.at[most], send_sem.at[0])
    wait_bytes(info_all.at[0, most], send_sem.at[1])
    wait_bytes(info_all.at[0], send_sem.at[2])
    wait_bytes(acts_cut, send_sem.at[3])


def spread(acts, info, w_enc, w_dec):
    dma = pltpu.SemaphoreType.DMA
    return pl.pallas_call(
        spread_kernel,
        out_shape=(
            jax.ShapeDtypeStruct((2, NP, ROWS, DS), BF16),
            jax.ShapeDtypeStruct((2, NP, 16, 128), BF16),
            jax.ShapeDtypeStruct((NP, LOCAL, DS), BF16),
            jax.ShapeDtypeStruct((NP, 48, DS), BF16),
        ),
        in_specs=[ANY] * 4,
        out_specs=(ANY, ANY, ANY, VMEM),
        scratch_shapes=[pltpu.VMEM((2, 48, D), BF16), pltpu.VMEM((ROWS, D), BF16),
                        pltpu.VMEM((NP, ROWS, DS), BF16), pltpu.VMEM((NP, 48, DS), BF16),
                        dma((3,)), dma((4,)), dma((NX,)), dma((1,)), dma((1,)), dma((1,))] + bring_sems(),
        compiler_params=pltpu.CompilerParams(collective_id=0, has_side_effects=True, vmem_limit_bytes=BIG),
        name="spread",
    )(acts, info, w_enc, w_dec)


def picks(info, c):
    half = c.astype(F32)
    slot = lax.broadcasted_iota(jnp.int32, (SLOTS, ROWS), 0).astype(F32)
    first = jnp.where(info[2:3] == half, info[0:1], -1.0)
    second = jnp.where(info[3:4] == half, info[1:2], -1.0)
    return ((slot == first) | (slot == second)).astype(F32).astype(BF16)


def low_half(shape):
    return lax.broadcasted_iota(jnp.int32, shape, 1) < BW


def lines_of(out):
    low = low_half((64, 128))
    a = jnp.where(low, out[0:64, 0:128], out[128:192, 0:128])
    b = jnp.where(low, out[64:128, 0:128], out[192:256, 0:128])
    d = jnp.concatenate([out[256:320, 128:192], out[320:384, 128:192]], axis=1)
    return a, b, d


def wide_of(a, b, d):
    low = low_half((64, 128))
    zero = jnp.zeros_like(a)
    top = jnp.concatenate(
        [jnp.where(low, a, zero), jnp.where(low, b, zero), jnp.where(low, zero, a), jnp.where(low, zero, b),
         zero, zero], axis=0)
    side = jnp.concatenate(
        [jnp.zeros((256, BW), a.dtype), d[:, 0:BW], d[:, BW:128]], axis=0)
    return jnp.concatenate([top, side], axis=1)


def store_by_slot(ref, s, value):
    ref[0, pl.ds(s, SLOTS, stride=64), :] = value[:, 0:128]
    ref[1, pl.ds(s, SLOTS, stride=64), :] = value[:, 128:256]


def load_owner(ref, o):
    rows = pl.ds(pl.multiple_of(o * 384, 384), 384)
    return jnp.concatenate([ref[0, rows, :], ref[1, rows, :]], axis=1)


def lines_out(lines, part, first, count):
    def body(s, _):
        part[s] = lines[pl.ds(s, LINES, stride=64), :].astype(part.dtype)
        return 0

    lax.fori_loop(first, first + count, body, 0, unroll=8)


def put_lines(lines, o, values):
    for k in range(3):
        lines[pl.ds(pl.multiple_of(o * 192 + k * 64, 64), 64), :] = values[k]


def get_lines(lines, o):
    return [lines[pl.ds(pl.multiple_of(o * 192 + k * 64, 64), 64), :] for k in range(3)]


def turn_in(source, lines):
    def body(s, _):
        lines[pl.ds(s, LINES, stride=64), :] = source[s].astype(F32)
        return 0

    lax.fori_loop(0, 64, body, 0, unroll=8)


CHUNKS = 4
S_STEP, O_STEP = 64 // CHUNKS, NP // CHUNKS
CHUNK_SEMS = pltpu.SemaphoreType.DMA((CHUNKS,))


def stream(src, dst, sems):
    k = src.shape[0] // CHUNKS
    return [pltpu.make_async_copy(src.at[pl.ds(i * k, k)], dst.at[pl.ds(i * k, k)], sems.at[i]) for i in range(CHUNKS)]


def start_all(*streams):
    for copies in streams:
        for copy in copies:
            copy.start()


def wait_all(*streams):
    for copies in streams:
        for copy in copies:
            copy.wait()


def encode_kernel(info_all, acts_hbm, enc_hbm, slots_hbm, part_hbm,
                  acts_all, enc_all, slots_out, part, slots, lines, a_sem, w_sem, s_sem, p_sem):
    _, _, c = place()
    acts_in, enc_in = stream(acts_hbm, acts_all, a_sem), stream(enc_hbm, enc_all, w_sem)
    out_slots, out_part = stream(slots_out, slots_hbm, s_sem), stream(part, part_hbm, p_sem)
    start_all(acts_in, enc_in)

    def expand(s, _):
        take = picks(info_all[s].astype(F32), c)
        store_by_slot(slots, s, jnp.dot(take, acts_all[s], preferred_element_type=F32))
        return 0

    def owner(o, _):
        inputs = load_owner(slots, o).astype(BF16)
        slots_out[o] = inputs
        put_lines(lines, o, lines_of(lax.dot_general(
            inputs, enc_all[o], (((1,), (1,)), ((), ())), preferred_element_type=F32)))
        return 0

    for i in range(CHUNKS):
        acts_in[i].wait()
        lax.fori_loop(i * S_STEP, (i + 1) * S_STEP, expand, 0, unroll=8)
    for i in range(CHUNKS):
        enc_in[i].wait()
        lax.fori_loop(i * O_STEP, (i + 1) * O_STEP, owner, 0, unroll=8)
        out_slots[i].start()
    for i in range(CHUNKS):
        lines_out(lines, part, i * S_STEP, S_STEP)
        out_part[i].start()
    wait_all(out_slots, out_part)


def encode(info_all, acts_all, enc_all):
    return pl.pallas_call(
        encode_kernel,
        out_shape=(
            jax.ShapeDtypeStruct((NP, 384, DS), BF16),
            jax.ShapeDtypeStruct((64, LINES, 128), F32),
        ),
        in_specs=[VMEM, ANY, ANY],
        out_specs=(ANY,) * 2,
        scratch_shapes=[pltpu.VMEM((64, ROWS, DS), BF16), pltpu.VMEM((NP, LOCAL, DS), BF16),
                        pltpu.VMEM((NP, 384, DS), BF16), pltpu.VMEM((64, LINES, 128), F32),
                        pltpu.VMEM((2, SLOTS * 64, 128), F32), pltpu.VMEM((LINES * 64, 128), F32)] + [CHUNK_SEMS] * 4,
        compiler_params=pltpu.CompilerParams(vmem_limit_bytes=BIG),
        name="encode",
    )(info_all, acts_all, enc_all)


def decode_kernel(info_all, codes, dec_hbm, recon_hbm, other_hbm, wide_hbm,
                  dec_all, recon, wide_out, slots, lines, w_sem, r_sem, o_sem, send_sem, recv_sem):
    y, p, c = place()
    pair = (y, p * 2 + 1 - c)
    barrier = pltpu.get_barrier_semaphore()
    pl.semaphore_signal(barrier, inc=1, device_id=pair, device_id_type=MESH)
    dec_in = stream(dec_hbm, dec_all, w_sem)
    out_recon, out_wide = stream(recon, recon_hbm, r_sem), stream(wide_out, wide_hbm, o_sem)
    start_all(dec_in)
    turn_in(codes, lines)

    def owner(o, _):
        wide = wide_of(*get_lines(lines, o)).astype(BF16)
        wide_out[o] = wide
        part = jnp.dot(wide, dec_all[o], preferred_element_type=F32)
        rows = pl.ds(pl.multiple_of(o * 384, 384), 384)
        slots[0, rows, :] = part[:, 0:128]
        slots[1, rows, :] = part[:, 128:256]
        return 0

    def gather(s, _):
        take = picks(info_all[s].astype(F32), c)
        part = jnp.concatenate(
            [slots[h, pl.ds(s, SLOTS, stride=64), :].astype(BF16) for h in range(2)], axis=1)
        recon[s] = lax.dot_general(
            take, part, (((0,), (0,)), ((), ())), preferred_element_type=F32).astype(BF16)
        return 0

    for i in range(CHUNKS):
        dec_in[i].wait()
        lax.fori_loop(i * O_STEP, (i + 1) * O_STEP, owner, 0, unroll=8)
        out_wide[i].start()
    pl.semaphore_wait(barrier, 1)
    sent = []
    for i in range(CHUNKS):
        lax.fori_loop(i * S_STEP, (i + 1) * S_STEP, gather, 0, unroll=8)
        out_recon[i].start()
        rows = pl.ds(i * S_STEP, S_STEP)
        sent.append(remote(recon.at[rows], other_hbm.at[rows], send_sem.at[i], recv_sem.at[i], pair))
        sent[i].start()
    wait_all(out_recon, out_wide, sent)


def decode(info_all, codes, dec_all):
    return pl.pallas_call(
        decode_kernel,
        out_shape=(
            jax.ShapeDtypeStruct((64, ROWS, DS), BF16),
            jax.ShapeDtypeStruct((64, ROWS, DS), BF16),
            jax.ShapeDtypeStruct((NP, 384, LOCAL), BF16),
        ),
        in_specs=[VMEM, VMEM, ANY],
        out_specs=(ANY,) * 3,
        scratch_shapes=[pltpu.VMEM((NP, LOCAL, DS), BF16), pltpu.VMEM((64, ROWS, DS), BF16),
                        pltpu.VMEM((NP, 384, LOCAL), BF16),
                        pltpu.VMEM((2, SLOTS * 64, 128), F32), pltpu.VMEM((LINES * 64, 128), F32)] + [CHUNK_SEMS] * 5,
        compiler_params=pltpu.CompilerParams(collective_id=4, has_side_effects=True, vmem_limit_bytes=BIG),
        name="decode",
    )(info_all, codes, dec_all)


def pack_owners(out, i, v0, v1):
    h, u = lax.div(i, 8), lax.rem(i, 8)
    for side in range(2):
        tile = slice(side * 128, side * 128 + 128)
        low, high = halves_of(v0[:, tile], v1[:, tile])
        out[2 * side, h, u] = low.astype(BF16)
        out[2 * side + 1, h, u] = high.astype(BF16)


OVER_ROWS = (((0,), (0,)), ((), ()))


def errors_kernel(info_all, b_dec, acts_hbm, mine_hbm, other_hbm, dec_hbm, wide_hbm, part, dec,
                  acts_all, mine, other, dec_all, wide, slots, lines, *sems):
    _, _, c = place()
    ins = [stream(src, dst, sem) for src, dst, sem in zip(
        (acts_hbm, mine_hbm, other_hbm, dec_hbm, wide_hbm), (acts_all, mine, other, dec_all, wide), sems)]
    for i in range(CHUNKS):
        start_all([copies[i] for copies in ins[0:3]])
    start_all(*ins[3:])

    def expand(s, _):
        recon = mine[s].astype(F32) + other[s].astype(F32)
        errors = (recon + b_dec[0:1] - acts_all[s].astype(F32)).astype(BF16)
        take = picks(info_all[s].astype(F32), c)
        store_by_slot(slots, s, jnp.dot(take, errors, preferred_element_type=F32))
        return 0

    def product(o):
        wanted = load_owner(slots, o).astype(BF16)
        grad = lax.dot_general(wanted, dec_all[o], (((1,), (1,)), ((), ())), preferred_element_type=F32)
        put_lines(lines, o, lines_of(grad))
        return lax.dot_general(wide[o], wanted, OVER_ROWS, preferred_element_type=F32)

    def owners(i, _):
        pack_owners(dec, i, product(2 * i), product(2 * i + 1))
        return 0

    for i in range(CHUNKS):
        wait_all([copies[i] for copies in ins[0:3]])
        lax.fori_loop(i * S_STEP, (i + 1) * S_STEP, expand, 0, unroll=8)
    for i in range(CHUNKS):
        wait_all([copies[i] for copies in ins[3:]])
        lax.fori_loop(i * O_STEP // 2, (i + 1) * O_STEP // 2, owners, 0, unroll=4)
    lines_out(lines, part, 0, 64)


def errors_of(info_all, acts_all, mine, other, b_dec, dec_all, wide, kind):
    return pl.pallas_call(
        errors_kernel,
        out_shape=(
            jax.ShapeDtypeStruct((64, LINES, 128), kind),
            jax.ShapeDtypeStruct((NY, 2, 8, LOCAL, 128), BF16),
        ),
        in_specs=[VMEM] * 2 + [ANY] * 5,
        out_specs=(VMEM,) * 2,
        scratch_shapes=[pltpu.VMEM((64, ROWS, DS), BF16)] * 3
        + [pltpu.VMEM((NP, LOCAL, DS), BF16), pltpu.VMEM((NP, 384, LOCAL), BF16),
           pltpu.VMEM((2, SLOTS * 64, 128), F32), pltpu.VMEM((LINES * 64, 128), F32)] + [CHUNK_SEMS] * 5,
        compiler_params=pltpu.CompilerParams(vmem_limit_bytes=BIG),
        name="errors",
    )(info_all, b_dec, acts_all, mine, other, dec_all, wide)


def enc_grads_kernel(g_all, inputs_hbm, enc, bias, inputs, lines, i_sem):
    inputs_in = stream(inputs_hbm, inputs, i_sem)
    start_all(inputs_in)
    turn_in(g_all, lines)

    def product(o):
        a, b, d = get_lines(lines, o)
        bias[o] = jnp.concatenate(
            [jnp.sum(a + b, axis=0, keepdims=True), jnp.sum(d, axis=0, keepdims=True), jnp.zeros((6, 128), F32)], axis=0)
        return lax.dot_general(wide_of(a, b, d).astype(BF16), inputs[o], OVER_ROWS, preferred_element_type=F32)

    def owners(i, _):
        pack_owners(enc, i, product(2 * i), product(2 * i + 1))
        return 0

    for i in range(CHUNKS):
        inputs_in[i].wait()
        lax.fori_loop(i * O_STEP // 2, (i + 1) * O_STEP // 2, owners, 0, unroll=4)


def enc_grads(g_all, inputs):
    return pl.pallas_call(
        enc_grads_kernel,
        out_shape=(
            jax.ShapeDtypeStruct((NY, 2, 8, LOCAL, 128), BF16),
            jax.ShapeDtypeStruct((NP, 8, 128), F32),
        ),
        in_specs=[VMEM, ANY],
        out_specs=(VMEM,) * 2,
        scratch_shapes=[pltpu.VMEM((NP, 384, DS), BF16), pltpu.VMEM((LINES * 64, 128), F32), CHUNK_SEMS],
        compiler_params=pltpu.CompilerParams(vmem_limit_bytes=BIG),
        name="enc_grads",
    )(g_all, inputs)


def meet_peers(y, p, c):
    side = lax.rem(lax.div(p, NZ), 2)

    def at(v, h):
        return (v, (p + (h - side) * NZ) * 2 + c)

    return side, lax.rem(y + 1, NY), lax.rem(y + NY - 1, NY), lax.rem(y + 2, NY), at


def meet_greet(y, p, c, barrier):
    side, up, down, far, at = meet_peers(y, p, c)
    for v in (up, down, far):
        for h in range(2):
            pl.semaphore_signal(barrier, inc=1, device_id=at(v, h), device_id_type=MESH)


MEET_PARTS = 3
MEET_ROWS = LOCAL // MEET_PARTS


def meet_rows(n):
    return pl.ds(n * MEET_ROWS, MEET_ROWS)


def meet_start(y, p, c, src, land, relay, send, recv):
    side, up, down, far, at = meet_peers(y, p, c)
    low, high = pl.ds(0, 4), pl.ds(4, 4)
    for n in range(MEET_PARTS):
        rows = meet_rows(n)
        remote(src.at[far, :, low, rows], relay.at[0, :, :, rows], send.at[0], recv.at[n, 0], at(up, side)).start()
        remote(src.at[far, :, high, rows], relay.at[1, :, :, rows], send.at[0], recv.at[n, 1], at(down, side)).start()
        for h in range(2):
            remote(src.at[up, h, high, rows], land.at[side, 1, high, rows], send.at[1], recv.at[n, 2], at(up, h)).start()
            remote(src.at[down, h, low, rows], land.at[side, 2, low, rows], send.at[1], recv.at[n, 2],
                   at(down, h)).start()
        pltpu.make_async_copy(src.at[y, side, :, rows], land.at[side, 0, :, rows], recv.at[n, 2]).start()
        remote(src.at[y, 1 - side, :, rows], land.at[side, 0, :, rows], send.at[1], recv.at[n, 2],
               at(y, 1 - side)).start()


def meet_merge(y, p, c, n, src, land, relay, merged, send, recv):
    side, up, down, far, at = meet_peers(y, p, c)
    rows = meet_rows(n)
    for k, (v, first) in enumerate(((up, 0), (down, 4))):
        wait_bytes(relay.at[k, :, :, rows], recv.at[n, k])
        for h in range(2):

            def add(i, _):
                merged[k, h, i, rows] = (
                    src[v, h, first + i, rows].astype(F32) + relay[k, h, i, rows].astype(F32)).astype(BF16)
                return 0

            lax.fori_loop(0, 4, add, 0)
            remote(merged.at[k, h, :, rows], land.at[side, 1 + k, pl.ds(first, 4), rows], send.at[1], recv.at[n, 2],
                   at(v, h)).start()


def meet_wait(n, land, recv):
    wait_bytes(land.at[:, :, :, meet_rows(n)], recv.at[n, 2])


def meet_sum(land, total, u, n):
    def tile(t, _):
        rows = pl.ds(pl.multiple_of(n * MEET_ROWS + t * 32, 32), 32)
        v = [land[e, 0, u, rows, :].astype(F32) + land[e, 1, u, rows, :].astype(F32) + land[e, 2, u, rows, :].astype(F32)
             for e in range(2)]
        low, high = halves_of(v[0], v[1])
        total[2 * u, rows, :], total[2 * u + 1, rows, :] = low.astype(BF16), high.astype(BF16)
        return 0

    lax.fori_loop(0, MEET_ROWS // 32, tile, 0)


def meet_end(land, relay, send):
    wait_bytes(relay, send.at[0])
    wait_bytes(land.at[0], send.at[1])
    wait_bytes(land.at[0, 0], send.at[1])
    wait_bytes(land.at[0, 0], send.at[1])


MEET_SCRATCH = [pltpu.VMEM((2, 3, 8, LOCAL, 128), BF16), pltpu.VMEM((2, 2, 4, LOCAL, 128), BF16),
                pltpu.VMEM((2, 2, 4, LOCAL, 128), BF16), pltpu.SemaphoreType.DMA((2,)), pltpu.SemaphoreType.DMA((MEET_PARTS, 3))]


def slope_of(v):
    return 0.5 * (1.0 + lax.erf(v * 0.7071067811865476)) + v * jnp.exp(-0.5 * v * v) * 0.3989422804014327


def exchange_kernel(forward, part, extra, *rest):
    if forward:
        (dec_cut, out_all, slope_out, dec_all, got, code, x_relay, x_merged, x_land, z_out, send_sem, xr_sem, xl_sem, recv_sem,
         line_sem, x_sem, far_sem, back_sem, w_send, w_recv, y_send, y_sem, w_far) = rest
    else:
        (dec, out_all, dec_total, got, code, x_relay, x_merged, x_land, z_out, send_sem, xr_sem, xl_sem, recv_sem,
         line_sem, x_sem, far_sem, back_sem, land, relay, merged, m_send, m_recv) = rest
    y, p, c = place()
    x, z = lax.div(p, NZ), lax.rem(p, NZ)
    barrier = pltpu.get_barrier_semaphore()

    right, left = lax.rem(x + 1, NX), lax.rem(x + NX - 1, NX)
    far = lax.rem(x + 2, NX)

    def in_line(i):
        return lax.rem(z + lax.rem(i, NZ), NZ), lax.rem(c + lax.div(i, NZ), 2)

    if forward:
        def greet(i, _):
            pl.semaphore_signal(barrier, inc=1, device_id=(y, shifted(p, i) * 2 + c), device_id_type=MESH)
            return 0

        def greet_other(w, _):
            pl.semaphore_signal(barrier, inc=1, device_id=(y, (x * NZ + w) * 2 + 1 - c), device_id_type=MESH)
            return 0

        lax.fori_loop(1, NP, greet, 0)
        lax.fori_loop(0, NZ, greet_other, 0)
        for step in (1, NY - 1):
            pl.semaphore_signal(barrier, inc=1, device_id=(lax.rem(y + step, NY), p * 2 + c), device_id_type=MESH)
        pl.semaphore_wait(barrier, NP - 1 + NZ + 2)
    else:
        def greet(i, _):
            w, h = in_line(i)
            pl.semaphore_signal(barrier, inc=1, device_id=(y, (x * NZ + w) * 2 + h), device_id_type=MESH)
            return 0

        lax.fori_loop(1, 2 * NZ, greet, 0)
        for v in (right, left):
            pl.semaphore_signal(barrier, inc=1, device_id=(y, (v * NZ + z) * 2 + c), device_id_type=MESH)
        meet_greet(y, p, c, barrier)
        pl.semaphore_wait(barrier, 23)

    def beside(v):
        return (y, (v * NZ + z) * 2 + c)

    def cut(ref, n):
        return ref.at[..., pl.ds(n * PART, PART), :]

    def rows_of(v, k, n):
        return part.at[k, pl.ds(v * NZ, NZ), pl.ds(n * PART, PART)]

    ways = ((right, left, 0), (left, right, 1))
    for n in range(PARTS):
        for to, _, k in ways:
            remote(rows_of(far, k, n), cut(x_relay.at[k], n), send_sem.at[0], xr_sem.at[n, k], beside(to)).start()
        for to, _, k in ways:
            remote(rows_of(to, 1 - k, n), cut(x_land.at[k, 1 - k], n), send_sem.at[1], xl_sem.at[n], beside(to)).start()
    if forward:
        bring(y, p, c, dec_cut, dec_all, w_send.at[0], w_recv)
    for n in range(PARTS):
        own = pl.ds(n * PART, PART)
        for to, _, k in ways:
            wait_bytes(cut(x_relay.at[k], n), xr_sem.at[n, k])

            def merge(w, _):
                x_merged[k, w, own] = (
                    part[k, to * NZ + w, own].astype(F32) + x_relay[k, w, own].astype(F32)).astype(part.dtype)
                return 0

            lax.fori_loop(0, NZ, merge, 0)
            remote(cut(x_merged.at[k], n), cut(x_land.at[k, k], n), send_sem.at[1], xl_sem.at[n], beside(to)).start()
    for n in range(PARTS):
        own = pl.ds(n * PART, PART)
        wait_bytes(cut(x_land, n), xl_sem.at[n])

        def z_send(i, _):
            w, h = in_line(i)
            z_out[h, w, own] = (part[h, x * NZ + w, own].astype(F32) + x_land[0, h, w, own].astype(F32)
                                + x_land[1, h, w, own].astype(F32))
            source, target = z_out.at[h, w, own], got.at[c, z, own]

            @pl.when(i > 0)
            def _():
                remote(source, target, send_sem.at[2], recv_sem.at[n], (y, (x * NZ + w) * 2 + h)).start()

            @pl.when(i == 0)
            def _():
                pltpu.make_async_copy(source, target, recv_sem.at[n]).start()

            return 0

        lax.fori_loop(0, 2 * NZ, z_send, 0)

    if forward:
        for i in range(NX):
            pass_own(y, p, c, dec_all, lax.rem(x - i + NX, NX), w_recv, y_send, y_sem)
    else:
        meet_start(y, p, c, dec, land, relay, m_send, m_recv)

    for n in range(PARTS):
        own = pl.ds(n * PART, PART)
        wait_bytes(cut(got, n), recv_sem.at[n])
        for h in range(2):
            for t in range(PART // 16):
                rows = pl.ds(n * PART + t * 16, 16)
                total = got[h, 0, rows, :]
                for q in range(1, NZ):
                    total = total + got[h, q, rows, :]
                if forward:
                    pre = total + extra[h, rows, :]
                    slope_out[h, rows, :] = slope_of(pre)
                    code[h, rows, :] = (pre * 0.5 * (1.0 + lax.erf(pre * 0.7071067811865476))).astype(BF16)
                else:
                    code[h, rows, :] = (total * extra[h, rows, :]).astype(BF16)
        pltpu.make_async_copy(code.at[c, own], out_all.at[c, p, own], line_sem.at[n]).start()

        def share(i, _):
            w, h = in_line(i)
            remote(code.at[h, own], out_all.at[c, p, own], back_sem.at[0], line_sem.at[n],
                   (y, (x * NZ + w) * 2 + h)).start()
            return 0

        lax.fori_loop(1, 2 * NZ, share, 0)

    if forward:
        for i in range(NX):
            pass_on(y, p, c, dec_all, lax.rem(x - i + NX, NX), y_send, y_sem, w_far)
    else:
        for n in range(MEET_PARTS):
            meet_merge(y, p, c, n, dec, land, relay, merged, m_send, m_recv)

    def line(v, k, n):
        return out_all.at[k, pl.ds(v * NZ, NZ), pl.ds(n * PART, PART)]

    for n in range(PARTS):
        wait_bytes(cut(out_all.at[:, pl.ds(0, NZ)], n), line_sem.at[n])
        for side, v in enumerate((right, left)):
            for k in (side, 1 - side):
                remote(line(x, k, n), line(x, k, n), back_sem.at[1], x_sem.at[n, side, k], beside(v)).start()
    for n in range(PARTS):
        for side, (v, to) in enumerate(((left, right), (right, left))):
            wait_bytes(line(v, side, n), x_sem.at[n, side, side])
            remote(line(v, side, n), line(v, side, n), back_sem.at[2], far_sem.at[n, side], beside(to)).start()
    if not forward:
        for n in range(MEET_PARTS):
            meet_wait(n, land, m_recv)

            def total_of(u, _):
                meet_sum(land, dec_total, u, n)
                return 0

            lax.fori_loop(0, 8, total_of, 0)
    for n in range(PARTS):
        for side, v in enumerate((left, right)):
            wait_bytes(line(v, 1 - side, n), x_sem.at[n, side, 1 - side])
            wait_bytes(line(v, 0, n), far_sem.at[n, side])
    wait_bytes(x_relay, send_sem.at[0])
    wait_bytes(x_land, send_sem.at[1])
    wait_bytes(got.at[0], send_sem.at[2])
    wait_bytes(got.at[0, pl.ds(0, NZ - 1)], send_sem.at[2])
    wait_bytes(out_all.at[0, pl.ds(0, 2 * NZ - 1)], back_sem.at[0])
    wait_bytes(out_all.at[0], back_sem.at[1])
    wait_bytes(out_all.at[0, pl.ds(0, 2 * NZ)], back_sem.at[2])
    if forward:
        bring_end(dec_cut, dec_all, w_send.at[0], y_send, w_far)
    else:
        meet_end(land, relay, m_send)


def exchange(forward, part, extra, *dec):
    dma = pltpu.SemaphoreType.DMA
    out = [jax.ShapeDtypeStruct((2, NP, LINES, 128), BF16)]
    if forward:
        out.append(jax.ShapeDtypeStruct((2, LINES, 128), F32))
        out.append(jax.ShapeDtypeStruct((NP, LOCAL, DS), BF16))
    else:
        out.append(jax.ShapeDtypeStruct((16, LOCAL, 128), BF16))
    return pl.pallas_call(
        functools.partial(exchange_kernel, forward),
        out_shape=tuple(out),
        in_specs=[VMEM] * (2 + len(dec)),
        out_specs=(VMEM, VMEM, ANY) if forward else (VMEM, VMEM),
        scratch_shapes=[pltpu.VMEM((2, NZ, LINES, 128), F32), pltpu.VMEM((2, LINES, 128), BF16),
                        pltpu.VMEM((2, NZ, LINES, 128), part.dtype), pltpu.VMEM((2, NZ, LINES, 128), part.dtype),
                        pltpu.VMEM((2, 2, NZ, LINES, 128), part.dtype), pltpu.VMEM((2, NZ, LINES, 128), F32),
                        dma((3,)), dma((PARTS, 2)), dma((PARTS,)), dma((PARTS,)), dma((PARTS,)), dma((PARTS, 2, 2)),
                        dma((PARTS, 2)), dma((3,))]
        + (bring_sems() if forward else MEET_SCRATCH),
        compiler_params=pltpu.CompilerParams(
            collective_id=1 if forward else 2, has_side_effects=True, vmem_limit_bytes=BIG),
        name="exchange_code" if forward else "exchange_grad",
    )(part.reshape(2, NP, LINES, 128), extra, *dec)


def deliver_kernel(enc, dec_total, bias, enc_out, dec_out, bias_out, bias_y, enc_total, b_send, b_recv,
                   send_sem, recv_sem, land, relay, merged, m_send, m_recv):
    y, p, c = place()
    x, z = lax.div(p, NZ), lax.rem(p, NZ)
    side = lax.rem(x, 2)
    barrier = pltpu.get_barrier_semaphore()

    def greet(i, _):
        pl.semaphore_signal(barrier, inc=1, device_id=(y, shifted(p, i) * 2 + c), device_id_type=MESH)
        return 0

    lax.fori_loop(1, NP, greet, 0)
    meet_greet(y, p, c, barrier)
    pl.semaphore_wait(barrier, NP - 1 + 6)

    here = pair_of(p)

    def to_owners(total, out, n, u, rows):
        for e in range(2):
            o = side * 2 * NZ + 2 * u + e

            @pl.when(o != p)
            def _():
                remote(total.at[2 * u + e, rows], out.at[here, rows], send_sem.at[n], recv_sem.at[n], (y, o * 2 + c)).start()

            @pl.when(o == p)
            def _():
                pltpu.make_async_copy(total.at[2 * u + e, rows], out.at[here, rows], recv_sem.at[n]).start()

    def turned(i):
        return lax.rem(i + lax.div(z, 2), 8)

    meet_start(y, p, c, enc, land, relay, m_send, m_recv)
    pltpu.make_async_copy(bias.at[p], bias_y.at[y], b_recv.at[0]).start()
    for j in range(1, NY):
        remote(bias.at[p], bias_y.at[y], b_send.at[0], b_recv.at[0], (lax.rem(y + j, NY), p * 2 + c)).start()

    def dec_owner(i, _):
        to_owners(dec_total, dec_out, 0, turned(i), pl.ds(0, LOCAL))
        return 0

    lax.fori_loop(0, 8, dec_owner, 0)
    for n in range(MEET_PARTS):
        meet_merge(y, p, c, n, enc, land, relay, merged, m_send, m_recv)
    for n in range(MEET_PARTS):
        meet_wait(n, land, m_recv)

        def enc_owner(i, _):
            u = turned(i)
            meet_sum(land, enc_total, u, n)
            to_owners(enc_total, enc_out, 1, u, meet_rows(n))
            return 0

        lax.fori_loop(0, 8, enc_owner, 0)
    wait_bytes(bias_y, b_recv.at[0])
    bias_out[...] = bias_y[0] + bias_y[1] + bias_y[2] + bias_y[3]
    wait_bytes(bias_y.at[pl.ds(0, NY - 1)], b_send.at[0])
    meet_end(land, relay, m_send)
    for n in range(2):
        wait_bytes(enc_total, recv_sem.at[n])
        wait_bytes(enc_total.at[pl.ds(0, 15)], send_sem.at[n])

        @pl.when(lax.div(x, 2) != side)
        def _():
            wait_bytes(enc_total.at[0], send_sem.at[n])


def deliver(enc, dec_total, bias):
    dma = pltpu.SemaphoreType.DMA
    return pl.pallas_call(
        deliver_kernel,
        out_shape=(
            jax.ShapeDtypeStruct((16, LOCAL, 128), BF16),
            jax.ShapeDtypeStruct((16, LOCAL, 128), BF16),
            jax.ShapeDtypeStruct((8, 128), F32),
        ),
        in_specs=[VMEM, VMEM, ANY],
        out_specs=(ANY, ANY, VMEM),
        scratch_shapes=[pltpu.VMEM((NY, 8, 128), F32), pltpu.VMEM((16, LOCAL, 128), BF16),
                        dma((1,)), dma((1,)), dma((2,)), dma((2,))] + MEET_SCRATCH,
        compiler_params=pltpu.CompilerParams(collective_id=3, has_side_effects=True, vmem_limit_bytes=BIG),
        name="deliver",
    )(enc, dec_total, bias)


def info_kernel(blocks, b_enc, out):
    numbers = blocks[...]
    first, second = numbers[0:1].astype(F32), numbers[1:2].astype(F32)
    square = (ROWS, ROWS)
    before = lax.broadcasted_iota(jnp.int32, square, 0) < lax.broadcasted_iota(jnp.int32, square, 1)
    first_down = jnp.transpose(jnp.broadcast_to(first, square))
    second_down = jnp.transpose(jnp.broadcast_to(second, square))

    def count(hit):
        return jnp.sum(jnp.where(hit, 1, 0), axis=0, keepdims=True)

    rank = jnp.concatenate([
        count((first_down == first) & before),
        count(first_down == second) + count((second_down == second) & before)], axis=0)
    owner = lax.div(numbers, 3)
    slot = (lax.div(owner, 2) * 3 + lax.rem(numbers, 3)) * 2 + rank
    bias = b_enc[...]
    line = jnp.concatenate(
        [bias[:, 0:128], bias[:, 0:128], jnp.concatenate([bias[:, 128:192], bias[:, 128:192]], axis=1)], axis=0)
    top = line.astype(BF16).astype(F32)
    middle = (line - top).astype(BF16).astype(F32)
    out[...] = jnp.concatenate(
        [slot.astype(F32), lax.rem(owner, 2).astype(F32), top, middle, line - top - middle, jnp.zeros((3, ROWS), F32)],
        axis=0).astype(BF16)


def info_of(blocks, b_enc):
    return pl.pallas_call(
        info_kernel,
        out_shape=jax.ShapeDtypeStruct((16, ROWS), BF16),
        in_specs=[VMEM] * 2,
        out_specs=VMEM,
        name="info",
    )(blocks.T, b_enc.reshape(1, LOCAL))


def shards(acts, blocks, w_enc, b_enc, w_dec, b_dec):
    l = lax.axis_index("latent")
    p = l // 2
    acts_all, info_all, enc_all, dec_cut = spread(acts, info_of(blocks, b_enc), w_enc.T, w_dec)
    acts_all = acts_all.reshape(64, ROWS, DS)
    info_all = info_all.reshape(64, 16, 128)
    inputs, part = encode(info_all, acts_all, enc_all)
    bias = info_all.astype(F32)
    bias = (bias[:, 4:7] + bias[:, 7:10] + bias[:, 10:13]).reshape(2, LINES, 128)
    codes, slope, dec_all = exchange(True, part, bias, dec_cut)
    recon, other, wide = decode(info_all, codes.reshape(64, LINES, 128), dec_all)
    my_b_dec = lax.dynamic_slice(b_dec.reshape(NY, D // NY), (0, pair_of(p) * 128 + p // NZ % 2 * 64), (NY, 64))
    my_b_dec = jnp.broadcast_to(my_b_dec.reshape(1, DS), (8, DS))
    g_part, dec = errors_of(info_all, acts_all, recon, other, my_b_dec, dec_all, wide, G_KIND)
    g_all, dec_total = exchange(False, g_part, slope, dec)
    enc, bias_sum = enc_grads(g_all.reshape(64, LINES, 128), inputs)
    enc_tiles, dec_tiles, lines = deliver(enc, dec_total, bias_sum)
    grad_b_enc = jnp.concatenate([lines[0], lines[1, 0:64] + lines[1, 64:128]])

    def whole(tiles):
        return tiles.transpose(1, 0, 2).reshape(LOCAL, D // NY).astype(F32)

    return whole(enc_tiles).T, grad_b_enc, whole(dec_tiles)


def solution(mesh):
    return jax.shard_map(
        shards,
        mesh=mesh,
        in_specs=(
            P(("dp", "latent"), None),
            P(("dp", "latent"), None),
            P(None, "latent"),
            P("latent"),
            P("latent", None),
            P(),
        ),
        out_specs=(P("dp", "latent"), P("latent"), P("latent", "dp")),
        check_vma=False,
    )
```

```python
import functools

import jax
import jax.numpy as jnp
from jax import lax
from jax.experimental import pallas as pl
from jax.experimental.pallas import tpu as pltpu
from jax.sharding import PartitionSpec as P

F32, BF16 = jnp.float32, jnp.bfloat16
MESH = pl.DeviceIdType.MESH
ANY = pl.BlockSpec(memory_space=pl.ANY)
VMEM = pl.BlockSpec(memory_space=pltpu.VMEM)

NY, NX, NZ = 4, 4, 8
NP = NX * NZ
ROWS, D, BW, LOCAL = 128, 8192, 64, 192
DS = D // NP
SLOTS = NP * 6
LINES = NP * 3
BIG = 60 * 1024 * 1024
G_KIND = F32
PARTS = 3
PART = LINES // PARTS


def place():
    y, l = lax.axis_index("dp"), lax.axis_index("latent")
    return y, lax.div(l, 2), lax.rem(l, 2)


def shifted(p, step):
    x = lax.rem(lax.div(p, NZ) + lax.div(step, NZ), NX)
    z = lax.rem(lax.rem(p, NZ) + lax.rem(step, NZ), NZ)
    return x * NZ + z


def pair_of(p):
    return lax.div(p, 2 * NZ) * NZ + lax.rem(p, NZ)


def remote(src, dst, send, recv, device):
    return pltpu.make_async_remote_copy(
        src_ref=src, dst_ref=dst, send_sem=send, recv_sem=recv, device_id=device, device_id_type=MESH
    )


def wait_bytes(ref, sem):
    pltpu.make_async_copy(ref, ref, sem).wait()


def halves_of(v0, v1):
    return (jnp.concatenate([v0[:, 0:BW], v1[:, 0:BW]], axis=1),
            jnp.concatenate([v0[:, BW:128], v1[:, BW:128]], axis=1))


def by_chip(src, dst):
    def tile(t, _):
        v = [src[:, pl.ds(pl.multiple_of(q * (D // NY) + t * 128, 128), 128)].astype(F32) for q in range(NY)]
        even, odd = zip(halves_of(v[0], v[1]), halves_of(v[2], v[3]))
        for side, (e, o) in enumerate(((even[0], odd[0]), (even[1], odd[1]))):
            chip = lax.div(t, NZ) * 2 * NZ + lax.rem(t, NZ)
            dst[chip, :, pl.ds(side * 128, 128)] = e.astype(BF16)
            dst[chip + NZ, :, pl.ds(side * 128, 128)] = o.astype(BF16)
        return 0

    lax.fori_loop(0, NP // 2, tile, 0)


def brought(y):
    return pl.ds(pl.multiple_of(y * 48, 16), 48)


def bring(y, p, c, cut, ref, send, recv):
    target = ref.at[p, brought(y), :]
    sem = recv.at[lax.div(p, NZ)]
    pltpu.make_async_copy(cut.at[p], target, sem).start()

    def body(i, _):
        q = shifted(p, i)
        remote(cut.at[q], target, send, sem, (y, q * 2 + c)).start()
        return 0

    lax.fori_loop(1, NP, body, 0)


def pass_own(y, p, c, ref, g, recv, y_send, y_sem):
    part = ref.at[pl.ds(g * NZ, NZ), brought(y), :]
    wait_bytes(part, recv.at[g])
    for side, step in enumerate((1, NY - 1)):
        remote(part, part, y_send.at[0], y_sem.at[side, g], (lax.rem(y + step, NY), p * 2 + c)).start()


def pass_on(y, p, c, ref, g, y_send, y_sem, far_sem):
    up, down = lax.rem(y + 1, NY), lax.rem(y + NY - 1, NY)
    for side, (v, to) in enumerate(((down, up), (up, down))):
        wait_bytes(ref.at[pl.ds(g * NZ, NZ), brought(v), :], y_sem.at[side, g])
        part = ref.at[pl.ds(g * NZ + side * (NZ // 2), NZ // 2), brought(v), :]
        remote(part, part, y_send.at[0], far_sem.at[side], (to, p * 2 + c)).start()


def bring_end(cut, ref, send, y_send, far_sem):
    for side in range(2):
        wait_bytes(cut.at[pl.ds(0, NP // 2)], far_sem.at[side])
    wait_bytes(ref.at[:, pl.ds(0, 144), :], y_send.at[0])
    wait_bytes(cut.at[pl.ds(0, NP - 1)], send)


def bring_sems():
    dma = pltpu.SemaphoreType.DMA
    return [dma((1,)), dma((NX,)), dma((1,)), dma((2, NX)), dma((2,))]


def spread_kernel(acts, info, w_enc, w_dec, acts_all, info_all, enc_all, dec_cut,
                  own, own_acts, acts_cut, enc_cut, local_sem, send_sem, acts_sem, info_sem,
                  pair_sem, info_pair_sem, w_send, w_recv, y_send, y_sem, far_sem):
    y, p, c = place()
    rows = brought(y)
    loads = [pltpu.make_async_copy(w_enc.at[rows, :], own.at[0], local_sem.at[0]),
             pltpu.make_async_copy(w_dec.at[rows, :], own.at[1], local_sem.at[1]),
             pltpu.make_async_copy(acts, own_acts, local_sem.at[2])]
    for load in loads:
        load.start()
    barrier = pltpu.get_barrier_semaphore()

    def greet(i, _):
        pl.semaphore_signal(barrier, inc=1, device_id=(y, shifted(p, i) * 2 + c), device_id_type=MESH)
        return 0

    lax.fori_loop(1, NP, greet, 0)
    pl.semaphore_signal(barrier, inc=1, device_id=(y, p * 2 + 1 - c), device_id_type=MESH)
    for j in range(1, NY):
        pl.semaphore_signal(barrier, inc=1, device_id=(lax.rem(y + j, NY), p * 2 + c), device_id_type=MESH)
    loads[0].wait()
    by_chip(own.at[0], enc_cut)
    pl.semaphore_wait(barrier, NP - 1 + 1 + NY - 1)

    mine = lax.div(p, NZ)
    pltpu.make_async_copy(info, info_all.at[c, p], info_sem.at[0]).start()

    bring(y, p, c, enc_cut, enc_all, w_send.at[0], w_recv)
    loads[2].wait()
    by_chip(own_acts, acts_cut)
    pltpu.make_async_copy(acts_cut.at[p], acts_all.at[c, p], acts_sem.at[mine]).start()

    def send_a(i, _):
        q = shifted(p, i)
        remote(info, info_all.at[c, p], send_sem.at[1], info_sem.at[0], (y, q * 2 + c)).start()
        remote(acts_cut.at[q], acts_all.at[c, p], send_sem.at[0], acts_sem.at[mine], (y, q * 2 + c)).start()
        return 0

    lax.fori_loop(1, NP, send_a, 0)

    loads[1].wait()
    by_chip(own.at[1], dec_cut)
    for i in range(NX + 1):
        if i < NX:
            pass_own(y, p, c, enc_all, lax.rem(mine - i + NX, NX), w_recv, y_send, y_sem)
        if i > 0:
            pass_on(y, p, c, enc_all, lax.rem(mine - i + 1 + NX, NX), y_send, y_sem, far_sem)
    pair = (y, p * 2 + 1 - c)
    wait_bytes(info_all.at[c], info_sem.at[0])
    remote(info_all.at[c], info_all.at[c], send_sem.at[2], info_pair_sem.at[0], pair).start()
    for i in range(NX):
        g = lax.rem(mine - i + NX, NX)
        part = acts_all.at[c, pl.ds(g * NZ, NZ)]
        wait_bytes(part, acts_sem.at[g])
        remote(part, part, send_sem.at[3], pair_sem.at[0], pair).start()

    wait_bytes(info_all.at[c], info_pair_sem.at[0])
    wait_bytes(acts_all.at[c], pair_sem.at[0])
    bring_end(enc_cut, enc_all, w_send.at[0], y_send, far_sem)
    most = pl.ds(0, NP - 1)
    wait_bytes(acts_cut.at[most], send_sem.at[0])
    wait_bytes(info_all.at[0, most], send_sem.at[1])
    wait_bytes(info_all.at[0], send_sem.at[2])
    wait_bytes(acts_cut, send_sem.at[3])


def spread(acts, info, w_enc, w_dec):
    dma = pltpu.SemaphoreType.DMA
    return pl.pallas_call(
        spread_kernel,
        out_shape=(
            jax.ShapeDtypeStruct((2, NP, ROWS, DS), BF16),
            jax.ShapeDtypeStruct((2, NP, 16, 128), BF16),
            jax.ShapeDtypeStruct((NP, LOCAL, DS), BF16),
            jax.ShapeDtypeStruct((NP, 48, DS), BF16),
        ),
        in_specs=[ANY] * 4,
        out_specs=(ANY, ANY, ANY, VMEM),
        scratch_shapes=[pltpu.VMEM((2, 48, D), BF16), pltpu.VMEM((ROWS, D), BF16),
                        pltpu.VMEM((NP, ROWS, DS), BF16), pltpu.VMEM((NP, 48, DS), BF16),
                        dma((3,)), dma((4,)), dma((NX,)), dma((1,)), dma((1,)), dma((1,))] + bring_sems(),
        compiler_params=pltpu.CompilerParams(collective_id=0, has_side_effects=True, vmem_limit_bytes=BIG),
        name="spread",
    )(acts, info, w_enc, w_dec)


def picks(info, c):
    half = c.astype(F32)
    slot = lax.broadcasted_iota(jnp.int32, (SLOTS, ROWS), 0).astype(F32)
    first = jnp.where(info[2:3] == half, info[0:1], -1.0)
    second = jnp.where(info[3:4] == half, info[1:2], -1.0)
    return ((slot == first) | (slot == second)).astype(F32).astype(BF16)


def low_half(shape):
    return lax.broadcasted_iota(jnp.int32, shape, 1) < BW


def lines_of(out):
    low = low_half((64, 128))
    a = jnp.where(low, out[0:64, 0:128], out[128:192, 0:128])
    b = jnp.where(low, out[64:128, 0:128], out[192:256, 0:128])
    d = jnp.concatenate([out[256:320, 128:192], out[320:384, 128:192]], axis=1)
    return a, b, d


def wide_of(a, b, d):
    low = low_half((64, 128))
    zero = jnp.zeros_like(a)
    top = jnp.concatenate(
        [jnp.where(low, a, zero), jnp.where(low, b, zero), jnp.where(low, zero, a), jnp.where(low, zero, b),
         zero, zero], axis=0)
    side = jnp.concatenate(
        [jnp.zeros((256, BW), a.dtype), d[:, 0:BW], d[:, BW:128]], axis=0)
    return jnp.concatenate([top, side], axis=1)


def store_by_slot(ref, s, value):
    ref[0, pl.ds(s, SLOTS, stride=64), :] = value[:, 0:128]
    ref[1, pl.ds(s, SLOTS, stride=64), :] = value[:, 128:256]


def load_owner(ref, o):
    rows = pl.ds(pl.multiple_of(o * 384, 384), 384)
    return jnp.concatenate([ref[0, rows, :], ref[1, rows, :]], axis=1)


def lines_out(lines, part, first, count):
    def body(s, _):
        part[s] = lines[pl.ds(s, LINES, stride=64), :].astype(part.dtype)
        return 0

    lax.fori_loop(first, first + count, body, 0, unroll=8)


def put_lines(lines, o, values):
    for k in range(3):
        lines[pl.ds(pl.multiple_of(o * 192 + k * 64, 64), 64), :] = values[k]


def get_lines(lines, o):
    return [lines[pl.ds(pl.multiple_of(o * 192 + k * 64, 64), 64), :] for k in range(3)]


def turn_in(source, lines):
    def body(s, _):
        lines[pl.ds(s, LINES, stride=64), :] = source[s].astype(F32)
        return 0

    lax.fori_loop(0, 64, body, 0, unroll=8)


CHUNKS = 4
S_STEP, O_STEP = 64 // CHUNKS, NP // CHUNKS
CHUNK_SEMS = pltpu.SemaphoreType.DMA((CHUNKS,))


def stream(src, dst, sems):
    k = src.shape[0] // CHUNKS
    return [pltpu.make_async_copy(src.at[pl.ds(i * k, k)], dst.at[pl.ds(i * k, k)], sems.at[i]) for i in range(CHUNKS)]


def start_all(*streams):
    for copies in streams:
        for copy in copies:
            copy.start()


def wait_all(*streams):
    for copies in streams:
        for copy in copies:
            copy.wait()


def encode_kernel(info_all, acts_hbm, enc_hbm, slots_hbm, part_hbm,
                  acts_all, enc_all, slots_out, part, slots, lines, a_sem, w_sem, s_sem, p_sem):
    _, _, c = place()
    acts_in, enc_in = stream(acts_hbm, acts_all, a_sem), stream(enc_hbm, enc_all, w_sem)
    out_slots, out_part = stream(slots_out, slots_hbm, s_sem), stream(part, part_hbm, p_sem)
    start_all(acts_in, enc_in)

    def expand(s, _):
        take = picks(info_all[s].astype(F32), c)
        store_by_slot(slots, s, jnp.dot(take, acts_all[s], preferred_element_type=F32))
        return 0

    def owner(o, _):
        inputs = load_owner(slots, o).astype(BF16)
        slots_out[o] = inputs
        put_lines(lines, o, lines_of(lax.dot_general(
            inputs, enc_all[o], (((1,), (1,)), ((), ())), preferred_element_type=F32)))
        return 0

    for i in range(CHUNKS):
        acts_in[i].wait()
        lax.fori_loop(i * S_STEP, (i + 1) * S_STEP, expand, 0, unroll=8)
    for i in range(CHUNKS):
        enc_in[i].wait()
        lax.fori_loop(i * O_STEP, (i + 1) * O_STEP, owner, 0, unroll=8)
        out_slots[i].start()
    for i in range(CHUNKS):
        lines_out(lines, part, i * S_STEP, S_STEP)
        out_part[i].start()
    wait_all(out_slots, out_part)


def encode(info_all, acts_all, enc_all):
    return pl.pallas_call(
        encode_kernel,
        out_shape=(
            jax.ShapeDtypeStruct((NP, 384, DS), BF16),
            jax.ShapeDtypeStruct((64, LINES, 128), F32),
        ),
        in_specs=[VMEM, ANY, ANY],
        out_specs=(ANY,) * 2,
        scratch_shapes=[pltpu.VMEM((64, ROWS, DS), BF16), pltpu.VMEM((NP, LOCAL, DS), BF16),
                        pltpu.VMEM((NP, 384, DS), BF16), pltpu.VMEM((64, LINES, 128), F32),
                        pltpu.VMEM((2, SLOTS * 64, 128), F32), pltpu.VMEM((LINES * 64, 128), F32)] + [CHUNK_SEMS] * 4,
        compiler_params=pltpu.CompilerParams(vmem_limit_bytes=BIG),
        name="encode",
    )(info_all, acts_all, enc_all)


def decode_kernel(info_all, codes, dec_hbm, recon_hbm, other_hbm, wide_hbm,
                  dec_all, recon, wide_out, slots, lines, w_sem, r_sem, o_sem, send_sem, recv_sem):
    y, p, c = place()
    pair = (y, p * 2 + 1 - c)
    barrier = pltpu.get_barrier_semaphore()
    pl.semaphore_signal(barrier, inc=1, device_id=pair, device_id_type=MESH)
    dec_in = stream(dec_hbm, dec_all, w_sem)
    out_recon, out_wide = stream(recon, recon_hbm, r_sem), stream(wide_out, wide_hbm, o_sem)
    start_all(dec_in)
    turn_in(codes, lines)

    def owner(o, _):
        wide = wide_of(*get_lines(lines, o)).astype(BF16)
        wide_out[o] = wide
        part = jnp.dot(wide, dec_all[o], preferred_element_type=F32)
        rows = pl.ds(pl.multiple_of(o * 384, 384), 384)
        slots[0, rows, :] = part[:, 0:128]
        slots[1, rows, :] = part[:, 128:256]
        return 0

    def gather(s, _):
        take = picks(info_all[s].astype(F32), c)
        part = jnp.concatenate(
            [slots[h, pl.ds(s, SLOTS, stride=64), :].astype(BF16) for h in range(2)], axis=1)
        recon[s] = lax.dot_general(
            take, part, (((0,), (0,)), ((), ())), preferred_element_type=F32).astype(BF16)
        return 0

    for i in range(CHUNKS):
        dec_in[i].wait()
        lax.fori_loop(i * O_STEP, (i + 1) * O_STEP, owner, 0, unroll=8)
        out_wide[i].start()
    pl.semaphore_wait(barrier, 1)
    sent = []
    for i in range(CHUNKS):
        lax.fori_loop(i * S_STEP, (i + 1) * S_STEP, gather, 0, unroll=8)
        out_recon[i].start()
        rows = pl.ds(i * S_STEP, S_STEP)
        sent.append(remote(recon.at[rows], other_hbm.at[rows], send_sem.at[i], recv_sem.at[i], pair))
        sent[i].start()
    wait_all(out_recon, out_wide, sent)


def decode(info_all, codes, dec_all):
    return pl.pallas_call(
        decode_kernel,
        out_shape=(
            jax.ShapeDtypeStruct((64, ROWS, DS), BF16),
            jax.ShapeDtypeStruct((64, ROWS, DS), BF16),
            jax.ShapeDtypeStruct((NP, 384, LOCAL), BF16),
        ),
        in_specs=[VMEM, VMEM, ANY],
        out_specs=(ANY,) * 3,
        scratch_shapes=[pltpu.VMEM((NP, LOCAL, DS), BF16), pltpu.VMEM((64, ROWS, DS), BF16),
                        pltpu.VMEM((NP, 384, LOCAL), BF16),
                        pltpu.VMEM((2, SLOTS * 64, 128), F32), pltpu.VMEM((LINES * 64, 128), F32)] + [CHUNK_SEMS] * 5,
        compiler_params=pltpu.CompilerParams(collective_id=4, has_side_effects=True, vmem_limit_bytes=BIG),
        name="decode",
    )(info_all, codes, dec_all)


def pack_owners(out, i, v0, v1):
    h, u = lax.div(i, 8), lax.rem(i, 8)
    for side in range(2):
        tile = slice(side * 128, side * 128 + 128)
        low, high = halves_of(v0[:, tile], v1[:, tile])
        out[2 * side, h, u] = low.astype(BF16)
        out[2 * side + 1, h, u] = high.astype(BF16)


OVER_ROWS = (((0,), (0,)), ((), ()))


def errors_kernel(info_all, b_dec, acts_hbm, mine_hbm, other_hbm, dec_hbm, wide_hbm, part, dec,
                  acts_all, mine, other, dec_all, wide, slots, lines, *sems):
    _, _, c = place()
    ins = [stream(src, dst, sem) for src, dst, sem in zip(
        (acts_hbm, mine_hbm, other_hbm, dec_hbm, wide_hbm), (acts_all, mine, other, dec_all, wide), sems)]
    for i in range(CHUNKS):
        start_all([copies[i] for copies in ins[0:3]])
    start_all(*ins[3:])

    def expand(s, _):
        recon = mine[s].astype(F32) + other[s].astype(F32)
        errors = (recon + b_dec[0:1] - acts_all[s].astype(F32)).astype(BF16)
        take = picks(info_all[s].astype(F32), c)
        store_by_slot(slots, s, jnp.dot(take, errors, preferred_element_type=F32))
        return 0

    def product(o):
        wanted = load_owner(slots, o).astype(BF16)
        grad = lax.dot_general(wanted, dec_all[o], (((1,), (1,)), ((), ())), preferred_element_type=F32)
        put_lines(lines, o, lines_of(grad))
        return lax.dot_general(wide[o], wanted, OVER_ROWS, preferred_element_type=F32)

    def owners(i, _):
        pack_owners(dec, i, product(2 * i), product(2 * i + 1))
        return 0

    for i in range(CHUNKS):
        wait_all([copies[i] for copies in ins[0:3]])
        lax.fori_loop(i * S_STEP, (i + 1) * S_STEP, expand, 0, unroll=8)
    for i in range(CHUNKS):
        wait_all([copies[i] for copies in ins[3:]])
        lax.fori_loop(i * O_STEP // 2, (i + 1) * O_STEP // 2, owners, 0, unroll=4)
    lines_out(lines, part, 0, 64)


def errors_of(info_all, acts_all, mine, other, b_dec, dec_all, wide, kind):
    return pl.pallas_call(
        errors_kernel,
        out_shape=(
            jax.ShapeDtypeStruct((64, LINES, 128), kind),
            jax.ShapeDtypeStruct((NY, 2, 8, LOCAL, 128), BF16),
        ),
        in_specs=[VMEM] * 2 + [ANY] * 5,
        out_specs=(VMEM,) * 2,
        scratch_shapes=[pltpu.VMEM((64, ROWS, DS), BF16)] * 3
        + [pltpu.VMEM((NP, LOCAL, DS), BF16), pltpu.VMEM((NP, 384, LOCAL), BF16),
           pltpu.VMEM((2, SLOTS * 64, 128), F32), pltpu.VMEM((LINES * 64, 128), F32)] + [CHUNK_SEMS] * 5,
        compiler_params=pltpu.CompilerParams(vmem_limit_bytes=BIG),
        name="errors",
    )(info_all, b_dec, acts_all, mine, other, dec_all, wide)


def enc_grads_kernel(g_all, inputs_hbm, enc, bias, inputs, lines, i_sem):
    inputs_in = stream(inputs_hbm, inputs, i_sem)
    start_all(inputs_in)
    turn_in(g_all, lines)

    def product(o):
        a, b, d = get_lines(lines, o)
        bias[o] = jnp.concatenate(
            [jnp.sum(a + b, axis=0, keepdims=True), jnp.sum(d, axis=0, keepdims=True), jnp.zeros((6, 128), F32)], axis=0)
        return lax.dot_general(wide_of(a, b, d).astype(BF16), inputs[o], OVER_ROWS, preferred_element_type=F32)

    def owners(i, _):
        pack_owners(enc, i, product(2 * i), product(2 * i + 1))
        return 0

    for i in range(CHUNKS):
        inputs_in[i].wait()
        lax.fori_loop(i * O_STEP // 2, (i + 1) * O_STEP // 2, owners, 0, unroll=4)


def enc_grads(g_all, inputs):
    return pl.pallas_call(
        enc_grads_kernel,
        out_shape=(
            jax.ShapeDtypeStruct((NY, 2, 8, LOCAL, 128), BF16),
            jax.ShapeDtypeStruct((NP, 8, 128), F32),
        ),
        in_specs=[VMEM, ANY],
        out_specs=(VMEM,) * 2,
        scratch_shapes=[pltpu.VMEM((NP, 384, DS), BF16), pltpu.VMEM((LINES * 64, 128), F32), CHUNK_SEMS],
        compiler_params=pltpu.CompilerParams(vmem_limit_bytes=BIG),
        name="enc_grads",
    )(g_all, inputs)


def meet_peers(y, p, c):
    side = lax.rem(lax.div(p, NZ), 2)

    def at(v, h):
        return (v, (p + (h - side) * NZ) * 2 + c)

    return side, lax.rem(y + 1, NY), lax.rem(y + NY - 1, NY), lax.rem(y + 2, NY), at


def meet_greet(y, p, c, barrier):
    side, up, down, far, at = meet_peers(y, p, c)
    for v in (up, down, far):
        for h in range(2):
            pl.semaphore_signal(barrier, inc=1, device_id=at(v, h), device_id_type=MESH)


MEET_PARTS = 3
MEET_ROWS = LOCAL // MEET_PARTS


def meet_rows(n):
    return pl.ds(n * MEET_ROWS, MEET_ROWS)


def meet_start(y, p, c, src, land, relay, send, recv):
    side, up, down, far, at = meet_peers(y, p, c)
    low, high = pl.ds(0, 4), pl.ds(4, 4)
    for n in range(MEET_PARTS):
        rows = meet_rows(n)
        remote(src.at[far, :, low, rows], relay.at[0, :, :, rows], send.at[0], recv.at[n, 0], at(up, side)).start()
        remote(src.at[far, :, high, rows], relay.at[1, :, :, rows], send.at[0], recv.at[n, 1], at(down, side)).start()
        for h in range(2):
            remote(src.at[up, h, high, rows], land.at[side, 1, high, rows], send.at[1], recv.at[n, 2], at(up, h)).start()
            remote(src.at[down, h, low, rows], land.at[side, 2, low, rows], send.at[1], recv.at[n, 2],
                   at(down, h)).start()
        pltpu.make_async_copy(src.at[y, side, :, rows], land.at[side, 0, :, rows], recv.at[n, 2]).start()
        remote(src.at[y, 1 - side, :, rows], land.at[side, 0, :, rows], send.at[1], recv.at[n, 2],
               at(y, 1 - side)).start()


def meet_merge(y, p, c, n, src, land, relay, merged, send, recv):
    side, up, down, far, at = meet_peers(y, p, c)
    rows = meet_rows(n)
    for k, (v, first) in enumerate(((up, 0), (down, 4))):
        wait_bytes(relay.at[k, :, :, rows], recv.at[n, k])
        for h in range(2):

            def add(i, _):
                merged[k, h, i, rows] = (
                    src[v, h, first + i, rows].astype(F32) + relay[k, h, i, rows].astype(F32)).astype(BF16)
                return 0

            lax.fori_loop(0, 4, add, 0)
            remote(merged.at[k, h, :, rows], land.at[side, 1 + k, pl.ds(first, 4), rows], send.at[1], recv.at[n, 2],
                   at(v, h)).start()


def meet_wait(n, land, recv):
    wait_bytes(land.at[:, :, :, meet_rows(n)], recv.at[n, 2])


def meet_sum(land, total, u, n):
    def tile(t, _):
        rows = pl.ds(pl.multiple_of(n * MEET_ROWS + t * 32, 32), 32)
        v = [land[e, 0, u, rows, :].astype(F32) + land[e, 1, u, rows, :].astype(F32) + land[e, 2, u, rows, :].astype(F32)
             for e in range(2)]
        low, high = halves_of(v[0], v[1])
        total[2 * u, rows, :], total[2 * u + 1, rows, :] = low.astype(BF16), high.astype(BF16)
        return 0

    lax.fori_loop(0, MEET_ROWS // 32, tile, 0)


def meet_end(land, relay, send):
    wait_bytes(relay, send.at[0])
    wait_bytes(land.at[0], send.at[1])
    wait_bytes(land.at[0, 0], send.at[1])
    wait_bytes(land.at[0, 0], send.at[1])


MEET_SCRATCH = [pltpu.VMEM((2, 3, 8, LOCAL, 128), BF16), pltpu.VMEM((2, 2, 4, LOCAL, 128), BF16),
                pltpu.VMEM((2, 2, 4, LOCAL, 128), BF16), pltpu.SemaphoreType.DMA((2,)), pltpu.SemaphoreType.DMA((MEET_PARTS, 3))]


def slope_of(v):
    return 0.5 * (1.0 + lax.erf(v * 0.7071067811865476)) + v * jnp.exp(-0.5 * v * v) * 0.3989422804014327


def beside_part(n):
    return range(n * NX // PARTS, (n + 1) * NX // PARTS)


def exchange_kernel(forward, part, extra, *rest):
    if forward:
        (dec_cut, out_all, slope_out, dec_all, got, code, x_relay, x_merged, x_land, z_out, send_sem, xr_sem, xl_sem, recv_sem,
         line_sem, x_sem, far_sem, back_sem, w_send, w_recv, y_send, y_sem, w_far) = rest
    else:
        (dec, out_all, dec_total, got, code, x_relay, x_merged, x_land, z_out, send_sem, xr_sem, xl_sem, recv_sem,
         line_sem, x_sem, far_sem, back_sem, land, relay, merged, m_send, m_recv) = rest
    y, p, c = place()
    x, z = lax.div(p, NZ), lax.rem(p, NZ)
    barrier = pltpu.get_barrier_semaphore()

    right, left = lax.rem(x + 1, NX), lax.rem(x + NX - 1, NX)
    far = lax.rem(x + 2, NX)

    def in_line(i):
        return lax.rem(z + lax.rem(i, NZ), NZ), lax.rem(c + lax.div(i, NZ), 2)

    if forward:
        def greet(i, _):
            pl.semaphore_signal(barrier, inc=1, device_id=(y, shifted(p, i) * 2 + c), device_id_type=MESH)
            return 0

        def greet_other(w, _):
            pl.semaphore_signal(barrier, inc=1, device_id=(y, (x * NZ + w) * 2 + 1 - c), device_id_type=MESH)
            return 0

        lax.fori_loop(1, NP, greet, 0)
        lax.fori_loop(0, NZ, greet_other, 0)
        for step in (1, NY - 1):
            pl.semaphore_signal(barrier, inc=1, device_id=(lax.rem(y + step, NY), p * 2 + c), device_id_type=MESH)
        pl.semaphore_wait(barrier, NP - 1 + NZ + 2)
    else:
        def greet(i, _):
            w, h = in_line(i)
            pl.semaphore_signal(barrier, inc=1, device_id=(y, (x * NZ + w) * 2 + h), device_id_type=MESH)
            return 0

        lax.fori_loop(1, 2 * NZ, greet, 0)
        for v in (right, left):
            pl.semaphore_signal(barrier, inc=1, device_id=(y, (v * NZ + z) * 2 + c), device_id_type=MESH)
        meet_greet(y, p, c, barrier)
        pl.semaphore_wait(barrier, 23)

    def beside(v):
        return (y, (v * NZ + z) * 2 + c)

    def cut(ref, n):
        return ref.at[..., pl.ds(n * PART, PART), :]

    def rows_of(v, k, n):
        return part.at[k, pl.ds(v * NZ, NZ), pl.ds(n * PART, PART)]

    ways = ((right, left, 0), (left, right, 1))
    for n in range(PARTS):
        for to, _, k in ways:
            remote(rows_of(far, k, n), cut(x_relay.at[k], n), send_sem.at[0], xr_sem.at[n, k], beside(to)).start()
        for to, _, k in ways:
            remote(rows_of(to, 1 - k, n), cut(x_land.at[k, 1 - k], n), send_sem.at[1], xl_sem.at[n], beside(to)).start()
    if forward:
        bring(y, p, c, dec_cut, dec_all, w_send.at[0], w_recv)
    for n in range(PARTS):
        own = pl.ds(n * PART, PART)
        for to, _, k in ways:
            wait_bytes(cut(x_relay.at[k], n), xr_sem.at[n, k])

            def merge(w, _):
                x_merged[k, w, own] = (
                    part[k, to * NZ + w, own].astype(F32) + x_relay[k, w, own].astype(F32)).astype(part.dtype)
                return 0

            lax.fori_loop(0, NZ, merge, 0)
            remote(cut(x_merged.at[k], n), cut(x_land.at[k, k], n), send_sem.at[1], xl_sem.at[n], beside(to)).start()
    for n in range(PARTS):
        own = pl.ds(n * PART, PART)
        wait_bytes(cut(x_land, n), xl_sem.at[n])

        def z_send(i, _):
            w, h = in_line(i)
            z_out[h, w, own] = (part[h, x * NZ + w, own].astype(F32) + x_land[0, h, w, own].astype(F32)
                                + x_land[1, h, w, own].astype(F32))
            source, target = z_out.at[h, w, own], got.at[c, z, own]

            @pl.when(i > 0)
            def _():
                remote(source, target, send_sem.at[2], recv_sem.at[n], (y, (x * NZ + w) * 2 + h)).start()

            @pl.when(i == 0)
            def _():
                pltpu.make_async_copy(source, target, recv_sem.at[n]).start()

            return 0

        lax.fori_loop(0, 2 * NZ, z_send, 0)
        if forward:
            for i in beside_part(n):
                pass_own(y, p, c, dec_all, lax.rem(x - i + NX, NX), w_recv, y_send, y_sem)

    if not forward:
        meet_start(y, p, c, dec, land, relay, m_send, m_recv)

    for n in range(PARTS):
        own = pl.ds(n * PART, PART)
        wait_bytes(cut(got, n), recv_sem.at[n])
        for h in range(2):
            for t in range(PART // 16):
                rows = pl.ds(n * PART + t * 16, 16)
                total = got[h, 0, rows, :]
                for q in range(1, NZ):
                    total = total + got[h, q, rows, :]
                if forward:
                    pre = total + extra[h, rows, :]
                    slope_out[h, rows, :] = slope_of(pre)
                    code[h, rows, :] = (pre * 0.5 * (1.0 + lax.erf(pre * 0.7071067811865476))).astype(BF16)
                else:
                    code[h, rows, :] = (total * extra[h, rows, :]).astype(BF16)
        pltpu.make_async_copy(code.at[c, own], out_all.at[c, p, own], line_sem.at[n]).start()

        def share(i, _):
            w, h = in_line(i)
            remote(code.at[h, own], out_all.at[c, p, own], back_sem.at[0], line_sem.at[n],
                   (y, (x * NZ + w) * 2 + h)).start()
            return 0

        lax.fori_loop(1, 2 * NZ, share, 0)
        if forward:
            for i in beside_part(n):
                pass_on(y, p, c, dec_all, lax.rem(x - i + NX, NX), y_send, y_sem, w_far)

    if not forward:
        for n in range(MEET_PARTS):
            meet_merge(y, p, c, n, dec, land, relay, merged, m_send, m_recv)

    def line(v, k, n):
        return out_all.at[k, pl.ds(v * NZ, NZ), pl.ds(n * PART, PART)]

    for n in range(PARTS):
        wait_bytes(cut(out_all.at[:, pl.ds(0, NZ)], n), line_sem.at[n])
        for side, v in enumerate((right, left)):
            for k in (side, 1 - side):
                remote(line(x, k, n), line(x, k, n), back_sem.at[1], x_sem.at[n, side, k], beside(v)).start()
    for n in range(PARTS):
        for side, (v, to) in enumerate(((left, right), (right, left))):
            wait_bytes(line(v, side, n), x_sem.at[n, side, side])
            remote(line(v, side, n), line(v, side, n), back_sem.at[2], far_sem.at[n, side], beside(to)).start()
    if not forward:
        for n in range(MEET_PARTS):
            meet_wait(n, land, m_recv)

            def total_of(u, _):
                meet_sum(land, dec_total, u, n)
                return 0

            lax.fori_loop(0, 8, total_of, 0)
    for n in range(PARTS):
        for side, v in enumerate((left, right)):
            wait_bytes(line(v, 1 - side, n), x_sem.at[n, side, 1 - side])
            wait_bytes(line(v, 0, n), far_sem.at[n, side])
    wait_bytes(x_relay, send_sem.at[0])
    wait_bytes(x_land, send_sem.at[1])
    wait_bytes(got.at[0], send_sem.at[2])
    wait_bytes(got.at[0, pl.ds(0, NZ - 1)], send_sem.at[2])
    wait_bytes(out_all.at[0, pl.ds(0, 2 * NZ - 1)], back_sem.at[0])
    wait_bytes(out_all.at[0], back_sem.at[1])
    wait_bytes(out_all.at[0, pl.ds(0, 2 * NZ)], back_sem.at[2])
    if forward:
        bring_end(dec_cut, dec_all, w_send.at[0], y_send, w_far)
    else:
        meet_end(land, relay, m_send)


def exchange(forward, part, extra, *dec):
    dma = pltpu.SemaphoreType.DMA
    out = [jax.ShapeDtypeStruct((2, NP, LINES, 128), BF16)]
    if forward:
        out.append(jax.ShapeDtypeStruct((2, LINES, 128), F32))
        out.append(jax.ShapeDtypeStruct((NP, LOCAL, DS), BF16))
    else:
        out.append(jax.ShapeDtypeStruct((16, LOCAL, 128), BF16))
    return pl.pallas_call(
        functools.partial(exchange_kernel, forward),
        out_shape=tuple(out),
        in_specs=[VMEM] * (2 + len(dec)),
        out_specs=(VMEM, VMEM, ANY) if forward else (VMEM, VMEM),
        scratch_shapes=[pltpu.VMEM((2, NZ, LINES, 128), F32), pltpu.VMEM((2, LINES, 128), BF16),
                        pltpu.VMEM((2, NZ, LINES, 128), part.dtype), pltpu.VMEM((2, NZ, LINES, 128), part.dtype),
                        pltpu.VMEM((2, 2, NZ, LINES, 128), part.dtype), pltpu.VMEM((2, NZ, LINES, 128), F32),
                        dma((3,)), dma((PARTS, 2)), dma((PARTS,)), dma((PARTS,)), dma((PARTS,)), dma((PARTS, 2, 2)),
                        dma((PARTS, 2)), dma((3,))]
        + (bring_sems() if forward else MEET_SCRATCH),
        compiler_params=pltpu.CompilerParams(
            collective_id=1 if forward else 2, has_side_effects=True, vmem_limit_bytes=BIG),
        name="exchange_code" if forward else "exchange_grad",
    )(part.reshape(2, NP, LINES, 128), extra, *dec)


def deliver_kernel(enc, dec_total, bias, enc_out, dec_out, bias_out, bias_y, enc_total, b_send, b_recv,
                   send_sem, recv_sem, land, relay, merged, m_send, m_recv):
    y, p, c = place()
    x, z = lax.div(p, NZ), lax.rem(p, NZ)
    side = lax.rem(x, 2)
    barrier = pltpu.get_barrier_semaphore()

    def greet(i, _):
        pl.semaphore_signal(barrier, inc=1, device_id=(y, shifted(p, i) * 2 + c), device_id_type=MESH)
        return 0

    lax.fori_loop(1, NP, greet, 0)
    meet_greet(y, p, c, barrier)
    pl.semaphore_wait(barrier, NP - 1 + 6)

    here = pair_of(p)

    def to_owners(total, out, n, u, rows):
        for e in range(2):
            o = side * 2 * NZ + 2 * u + e

            @pl.when(o != p)
            def _():
                remote(total.at[2 * u + e, rows], out.at[here, rows], send_sem.at[n], recv_sem.at[n], (y, o * 2 + c)).start()

            @pl.when(o == p)
            def _():
                pltpu.make_async_copy(total.at[2 * u + e, rows], out.at[here, rows], recv_sem.at[n]).start()

    def turned(i):
        return lax.rem(i + lax.div(z, 2), 8)

    meet_start(y, p, c, enc, land, relay, m_send, m_recv)
    pltpu.make_async_copy(bias.at[p], bias_y.at[y], b_recv.at[0]).start()
    for j in range(1, NY):
        remote(bias.at[p], bias_y.at[y], b_send.at[0], b_recv.at[0], (lax.rem(y + j, NY), p * 2 + c)).start()

    def dec_owner(i, _):
        to_owners(dec_total, dec_out, 0, turned(i), pl.ds(0, LOCAL))
        return 0

    lax.fori_loop(0, 8, dec_owner, 0)
    for n in range(MEET_PARTS):
        meet_merge(y, p, c, n, enc, land, relay, merged, m_send, m_recv)
    for n in range(MEET_PARTS):
        meet_wait(n, land, m_recv)

        def enc_owner(i, _):
            u = turned(i)
            meet_sum(land, enc_total, u, n)
            to_owners(enc_total, enc_out, 1, u, meet_rows(n))
            return 0

        lax.fori_loop(0, 8, enc_owner, 0)
    wait_bytes(bias_y, b_recv.at[0])
    total = bias_y[0] + bias_y[1] + bias_y[2] + bias_y[3]
    bias_out[...] = jnp.concatenate([total[0:1], total[1:2, 0:BW] + total[1:2, BW:128]], axis=1)
    wait_bytes(bias_y.at[pl.ds(0, NY - 1)], b_send.at[0])
    meet_end(land, relay, m_send)
    for n in range(2):
        wait_bytes(enc_total, recv_sem.at[n])
        wait_bytes(enc_total.at[pl.ds(0, 15)], send_sem.at[n])

        @pl.when(lax.div(x, 2) != side)
        def _():
            wait_bytes(enc_total.at[0], send_sem.at[n])


def deliver(enc, dec_total, bias):
    dma = pltpu.SemaphoreType.DMA
    return pl.pallas_call(
        deliver_kernel,
        out_shape=(
            jax.ShapeDtypeStruct((16, LOCAL, 128), BF16),
            jax.ShapeDtypeStruct((16, LOCAL, 128), BF16),
            jax.ShapeDtypeStruct((1, LOCAL), F32),
        ),
        in_specs=[VMEM, VMEM, ANY],
        out_specs=(ANY, ANY, VMEM),
        scratch_shapes=[pltpu.VMEM((NY, 8, 128), F32), pltpu.VMEM((16, LOCAL, 128), BF16),
                        dma((1,)), dma((1,)), dma((2,)), dma((2,))] + MEET_SCRATCH,
        compiler_params=pltpu.CompilerParams(collective_id=3, has_side_effects=True, vmem_limit_bytes=BIG),
        name="deliver",
    )(enc, dec_total, bias)


def info_kernel(blocks, b_enc, out):
    numbers = blocks[...]
    first, second = numbers[0:1].astype(F32), numbers[1:2].astype(F32)
    square = (ROWS, ROWS)
    before = lax.broadcasted_iota(jnp.int32, square, 0) < lax.broadcasted_iota(jnp.int32, square, 1)
    first_down = jnp.transpose(jnp.broadcast_to(first, square))
    second_down = jnp.transpose(jnp.broadcast_to(second, square))

    def count(hit):
        return jnp.sum(jnp.where(hit, 1, 0), axis=0, keepdims=True)

    rank = jnp.concatenate([
        count((first_down == first) & before),
        count(first_down == second) + count((second_down == second) & before)], axis=0)
    owner = lax.div(numbers, 3)
    slot = (lax.div(owner, 2) * 3 + lax.rem(numbers, 3)) * 2 + rank
    bias = b_enc[...]
    line = jnp.concatenate(
        [bias[:, 0:128], bias[:, 0:128], jnp.concatenate([bias[:, 128:192], bias[:, 128:192]], axis=1)], axis=0)
    top = line.astype(BF16).astype(F32)
    middle = (line - top).astype(BF16).astype(F32)
    out[...] = jnp.concatenate(
        [slot.astype(F32), lax.rem(owner, 2).astype(F32), top, middle, line - top - middle, jnp.zeros((3, ROWS), F32)],
        axis=0).astype(BF16)


def info_of(blocks, b_enc):
    return pl.pallas_call(
        info_kernel,
        out_shape=jax.ShapeDtypeStruct((16, ROWS), BF16),
        in_specs=[VMEM] * 2,
        out_specs=VMEM,
        name="info",
    )(blocks.T, b_enc.reshape(1, LOCAL))


def shards(acts, blocks, w_enc, b_enc, w_dec, b_dec):
    l = lax.axis_index("latent")
    p = l // 2
    acts_all, info_all, enc_all, dec_cut = spread(acts, info_of(blocks, b_enc), w_enc.T, w_dec)
    acts_all = acts_all.reshape(64, ROWS, DS)
    info_all = info_all.reshape(64, 16, 128)
    inputs, part = encode(info_all, acts_all, enc_all)
    bias = info_all.astype(F32)
    bias = (bias[:, 4:7] + bias[:, 7:10] + bias[:, 10:13]).reshape(2, LINES, 128)
    codes, slope, dec_all = exchange(True, part, bias, dec_cut)
    recon, other, wide = decode(info_all, codes.reshape(64, LINES, 128), dec_all)
    my_b_dec = lax.dynamic_slice(b_dec.reshape(NY, D // NY), (0, pair_of(p) * 128 + p // NZ % 2 * 64), (NY, 64))
    my_b_dec = jnp.broadcast_to(my_b_dec.reshape(1, DS), (8, DS))
    g_part, dec = errors_of(info_all, acts_all, recon, other, my_b_dec, dec_all, wide, G_KIND)
    g_all, dec_total = exchange(False, g_part, slope, dec)
    enc, bias_sum = enc_grads(g_all.reshape(64, LINES, 128), inputs)
    enc_tiles, dec_tiles, lines = deliver(enc, dec_total, bias_sum)
    grad_b_enc = lines.reshape(LOCAL)

    def whole(tiles):
        return tiles.transpose(1, 0, 2).reshape(LOCAL, D // NY).astype(F32)

    return whole(enc_tiles).T, grad_b_enc, whole(dec_tiles)


def solution(mesh):
    return jax.shard_map(
        shards,
        mesh=mesh,
        in_specs=(
            P(("dp", "latent"), None),
            P(("dp", "latent"), None),
            P(None, "latent"),
            P("latent"),
            P("latent", None),
            P(),
        ),
        out_specs=(P("dp", "latent"), P("latent"), P("latent", "dp")),
        check_vma=False,
    )
```
